512 devices in a mesh: inst: 64 (over z_lo, y, core), tensor: 8 (over z_hi, x).
Axes of the slice: x: 4, y: 8, z: 8 (z_hi: 2, z_lo: 4; z = z_hi * 4 + z_lo), core: 2. Of those that a mesh axis runs over, the one named last changes fastest.
Arguments:
- query_first: bfloat16 [64, 8, 8192], P('inst', None, 'tensor')
- query_second: bfloat16 [64, 8, 8192], P('inst', None, 'tensor')
- hidden_first: bfloat16 [64, 8, 8192], P('inst', None, 'tensor'), may hold values from -6 to 6
- hidden_second: bfloat16 [64, 8, 8192], P('inst', None, 'tensor'), may hold values from -6 to 6
- fresh_first: bfloat16 [64, 8, 2, 1024], P('inst', None, None, 'tensor')
- fresh_second: bfloat16 [64, 8, 2, 1024], P('inst', None, None, 'tensor')
- kv_cache: bfloat16 [64, 8, 2, 1024, 1024], P('inst', None, None, None, 'tensor')
- adapters: bfloat16 [64, 4, 4, 16, 8192], P('inst', None, None, None, 'tensor')
- lengths: int32 [64, 8], replicated, may hold values from 1 to 1022, as said below
- adapter_ids: int32 [64, 8], replicated, may hold values from 0 to 3
- move_counts: int32 [64], replicated, may hold values from 0 to 4, as said below
- move_from: int32 [64, 4], replicated, may hold values from 0 to 7, as said below
- move_to: int32 [64, 4], replicated, may hold values from 0 to 7, as said below
Outputs:
- attn_first: bfloat16 [64, 8, 8192], P('inst', None, 'tensor')
- delta_first: bfloat16 [64, 8, 8192], P('inst', None, 'tensor')
- attn_second: bfloat16 [64, 8, 8192], P('inst', None, 'tensor')
- delta_second: bfloat16 [64, 8, 8192], P('inst', None, 'tensor')
The draws below stay inside these ranges and needn't reach their ends.
Inputs may be any that keep to these rules, and one draw needn't show every extreme that they name: `move_counts`: of two partners i and i xor 64/2 at most one has a nonzero count; some instance hands over 4. `move_from`: the entries of one row are distinct slots. `move_to`: the entries of one row are distinct slots. `lengths`: some slot holds 1022 tokens.
All inputs are finite; a program needn't handle non-finite values.
Results may differ from the reference program's by a relative error of at most 0.013.
Values may be sent and summed in bfloat16 or wider, within the bound.
No kernel may reach another device: no remote copies, remote signals or barrier semaphores. Data moves between devices by JAX's collectives and lax.ppermute only.
A program may use at most 64 MiB of HBM per device.

```python
import math
import jax
import jax.numpy as jnp
from jax import lax

D = 8192
HEAD = 128
RANK = 16
SLOTS = 8
CACHE = 1024
POOL = 4
MOVES = 4
INSTANCES = 64
QUERY_WIDTH = 8192
KV_WIDTH = 1024
N_INST = 64


def pair_hot(key):
    members = jax.random.randint(key, (INSTANCES // 2,), 0, 2)
    instance = jnp.arange(INSTANCES)
    upper = (instance >= INSTANCES // 2).astype(jnp.int32)
    return members[instance % (INSTANCES // 2)] == upper


def draw_lengths(key, part):
    hot = pair_hot(key)
    key = jax.random.fold_in(key, 11)
    key_values, key_top, key_low = jax.random.split(key, 3)
    lowest = jnp.broadcast_to(jnp.where(hot, CACHE // 2, 1)[:, None], (INSTANCES, SLOTS))
    values = jax.random.randint(key_values, (INSTANCES, SLOTS), lowest, CACHE - 1).reshape(-1)
    entries = INSTANCES * SLOTS
    flat_iota = jnp.arange(entries)
    top_at = jax.random.randint(key_top, (), 0, entries)
    values = jnp.where(flat_iota == top_at, CACHE - 2, values)
    low_at = (top_at + 1 + jax.random.randint(key_low, (), 0, entries - 1)) % entries
    values = jnp.where(flat_iota == low_at, 1, values)
    return values.reshape(INSTANCES, SLOTS).astype(jnp.int32)


def draw_move_counts(key, part):
    hot = pair_hot(key)
    key = jax.random.fold_in(key, 12)
    key_values, key_pick = jax.random.split(key)
    values = jax.random.randint(key_values, (INSTANCES,), MOVES - MOVES // 4, MOVES + 1)
    values = jnp.where(hot, values, 0)
    picked = jax.random.randint(key_pick, (), 0, INSTANCES // 2)
    filled = hot & (jnp.arange(INSTANCES) % (INSTANCES // 2) == picked)
    return jnp.where(filled, MOVES, values).astype(jnp.int32)


def permuted_rows(key):
    keys = jax.random.split(key, INSTANCES)
    orders = jax.vmap(lambda single: jax.random.permutation(single, SLOTS))(keys)
    return orders[:, :MOVES].astype(jnp.int32)


def draw_move_from(key, part):
    key = jax.random.fold_in(key, 13)
    return permuted_rows(key)


def draw_move_to(key, part):
    key = jax.random.fold_in(key, 14)
    return permuted_rows(key)


def draw_query_first(key, part):
    key = jax.random.fold_in(key, 21)
    return jax.random.normal(key, (INSTANCES, SLOTS, QUERY_WIDTH), jnp.float32).astype(jnp.bfloat16)


def draw_query_second(key, part):
    key = jax.random.fold_in(key, 22)
    return jax.random.normal(key, (INSTANCES, SLOTS, QUERY_WIDTH), jnp.float32).astype(jnp.bfloat16)


def fresh_tokens(key):
    return jax.random.normal(jax.random.fold_in(key, 99), (INSTANCES, SLOTS, 2, KV_WIDTH), jnp.float32).astype(jnp.bfloat16)


def draw_fresh_first(key, part):
    return fresh_tokens(jax.random.fold_in(key, 23))


def draw_fresh_second(key, part):
    return fresh_tokens(jax.random.fold_in(key, 24))


def draw_kv_cache(key, part):
    key = jax.random.fold_in(key, 25)
    return jax.random.normal(key, (INSTANCES, SLOTS, 2, CACHE, KV_WIDTH), jnp.float32).astype(jnp.bfloat16)


def draw_adapters(key, part):
    key = jax.random.fold_in(key, 26)
    factors = jnp.array([D ** (-0.5), RANK ** (-0.5), QUERY_WIDTH ** (-0.5), RANK ** (-0.5)], jnp.float32)
    factors = factors[None, None, :, None, None]
    base = jax.random.normal(key, (INSTANCES, POOL, 4, RANK, D), jnp.float32)
    return (base * factors).astype(jnp.bfloat16)


def plant(result, own_key, low, high):
    longest = result.shape.index(max(result.shape))
    spots = []
    for shift in (0, 1):
        where = [jax.random.randint(jax.random.fold_in(own_key, axis), (), 0, length) for axis, length in enumerate(result.shape)]
        where[longest] = (where[longest] + shift) % result.shape[longest]
        spots.append(tuple(where))
    return result.at[spots[0]].set(low).at[spots[1]].set(high)


def steps_of(rng, shape, cuts, smallest, top_value):
    def one(axis_at, parts):
        heights = jax.random.uniform(jax.random.fold_in(jax.random.fold_in(rng, 6), axis_at), (parts,), jnp.float32, smallest / len(cuts), top_value / len(cuts))
        return jnp.repeat(jnp.exp(heights), shape[axis_at] // parts).reshape((-1,) + (1,) * (len(shape) - axis_at - 1))

    level = one(*cuts[0])
    for cut in cuts[1:]:
        level = level * one(*cut)
    return level


def scatter_about(stream_key, extent, deviation, most, shards=(), held_as=jnp.bfloat16):
    values = jax.random.normal(stream_key, extent, jnp.float32) * deviation
    if len(shards) > 0:
        values = steps_of(stream_key, extent, shards, -0.22, 0.18) * values
    return jnp.clip(values, min=-most, max=most).astype(held_as)


def setup_inputs(seed: int = 0) -> dict:
    seeds = jax.random.split(jax.random.key(seed), 14)
    return {
        "query_first": draw_query_first(jax.random.fold_in(seeds[13], 71), 0),
        "query_second": draw_query_second(jax.random.fold_in(seeds[13], 71), 0),
        "hidden_first": scatter_about(seeds[2], (INSTANCES, SLOTS, D), 1.0, 6.0, ((0, 64), (2, 8))),
        "hidden_second": scatter_about(seeds[3], (INSTANCES, SLOTS, D), 1.0, 6.0, ((0, 64), (2, 8))),
        "fresh_first": draw_fresh_first(jax.random.fold_in(seeds[13], 71), 0),
        "fresh_second": draw_fresh_second(jax.random.fold_in(seeds[13], 71), 0),
        "kv_cache": draw_kv_cache(jax.random.fold_in(seeds[13], 71), 0),
        "adapters": draw_adapters(jax.random.fold_in(seeds[13], 71), 0),
        "lengths": draw_lengths(jax.random.fold_in(seeds[13], 71), 0),
        "adapter_ids": plant(jax.random.randint(seeds[9], (INSTANCES, SLOTS), 0, POOL), jax.random.fold_in(seeds[9], 1), 0, POOL - 1).astype(jnp.int32),
        "move_counts": draw_move_counts(jax.random.fold_in(seeds[13], 71), 0),
        "move_from": draw_move_from(jax.random.fold_in(seeds[13], 71), 0),
        "move_to": draw_move_to(jax.random.fold_in(seeds[13], 71), 0),
    }


masked_score = -1e+30

def attend(queries, stored_keys, stored_values, visible, extra_keys, extra_values, extra_visible):
    row_count = queries.shape[0]
    kv_heads = stored_keys.shape[-1] // HEAD
    group_size = queries.shape[-1] // stored_keys.shape[-1]
    scaling = 1.0 / math.sqrt(HEAD)
    grouped = queries.astype(jnp.float32).reshape(row_count, kv_heads, group_size, HEAD)
    keys_main = stored_keys.astype(jnp.float32).reshape(row_count, -1, kv_heads, HEAD)
    values_main = stored_values.astype(jnp.float32).reshape(row_count, -1, kv_heads, HEAD)
    keys_more = extra_keys.astype(jnp.float32).reshape(row_count, -1, kv_heads, HEAD)
    values_more = extra_values.astype(jnp.float32).reshape(row_count, -1, kv_heads, HEAD)
    scores_main = jnp.einsum('rkgd,rckd->rkgc', grouped, keys_main) * scaling
    scores_more = jnp.einsum('rkgd,rekd->rkge', grouped, keys_more) * scaling
    scores_main = jnp.where(visible[:, None, None, :], scores_main, masked_score)
    scores_more = jnp.where(extra_visible[:, None, None, :], scores_more, masked_score)
    largest = jnp.maximum(lax.optimization_barrier(jnp.max(scores_main, -1)), lax.optimization_barrier(jnp.max(scores_more, -1)))[..., None]
    weights_main = jnp.exp(scores_main - largest)
    weights_more = jnp.exp(scores_more - largest)
    denominator = lax.optimization_barrier(jnp.sum(weights_main, -1, keepdims=True)) + lax.optimization_barrier(jnp.sum(weights_more, -1, keepdims=True))
    probs_main = (weights_main / denominator).astype(jnp.bfloat16)
    probs_more = (weights_more / denominator).astype(jnp.bfloat16)
    mixed = jnp.einsum('rkgc,rckd->rkgd', probs_main.astype(jnp.float32), values_main)
    mixed = mixed + jnp.einsum('rkge,rekd->rkgd', probs_more.astype(jnp.float32), values_more)
    return mixed.reshape(row_count, -1).astype(jnp.bfloat16)

def query_section(query_base, hidden, row_tables):
    rank_part = jnp.einsum('rd,rkd->rk', hidden.astype(jnp.float32), row_tables[:, 0].astype(jnp.float32))
    rank_value = rank_part.astype(jnp.bfloat16)
    update = jnp.einsum('rk,rkd->rd', rank_value.astype(jnp.float32), row_tables[:, 1].astype(jnp.float32))
    return (query_base.astype(jnp.float32) + update).astype(jnp.bfloat16)

def output_section(attended, row_tables):
    rank_part = jnp.einsum('rd,rkd->rk', attended.astype(jnp.float32), row_tables[:, 2].astype(jnp.float32))
    rank_value = rank_part.astype(jnp.bfloat16)
    update = jnp.einsum('rk,rkd->rd', rank_value.astype(jnp.float32), row_tables[:, 3].astype(jnp.float32))
    return update.astype(jnp.bfloat16)

def reference(query_first, query_second, hidden_first, hidden_second, fresh_first, fresh_second, kv_cache, adapters, lengths, adapter_ids, move_counts, move_from, move_to):
    slot_iota = jnp.arange(SLOTS, dtype=jnp.int32)
    positions = jnp.arange(CACHE, dtype=jnp.int32)
    move_iota = jnp.arange(MOVES, dtype=jnp.int32)

    def per_instance(index):
        partner = jnp.bitwise_xor(index, N_INST // 2).astype(jnp.int32)
        own_store = kv_cache[index]
        other_store = kv_cache[partner]
        own_tables = adapters[index][adapter_ids[index]]
        own_length = lengths[index]
        fresh_one = fresh_first[index]
        queries_one = query_section(query_first[index], hidden_first[index], own_tables)
        attended_one = attend(queries_one, own_store[:, 0], own_store[:, 1], positions[None, :] < own_length[:, None], fresh_one[:, 0:1], fresh_one[:, 1:2], jnp.ones((SLOTS, 1), bool))
        update_one = output_section(attended_one, own_tables)
        arrive = (move_to[partner][None, :] == slot_iota[:, None]) & (move_iota < move_counts[partner])[None, :]
        incoming = jnp.any(arrive, 1)
        which_move = lax.optimization_barrier(jnp.sum(jnp.where(arrive, move_iota[None, :], 0), 1)).astype(jnp.int32)
        source_slot = move_from[partner][which_move].astype(jnp.int32)
        vacated = jnp.any((move_from[index][None, :] == slot_iota[:, None]) & (move_iota < move_counts[index])[None, :], 1)
        store_two = jnp.where(incoming[:, None, None, None], other_store[source_slot], own_store)
        fresh_prior = jnp.where(incoming[:, None, None], fresh_first[partner][source_slot], fresh_one)
        prior_length = jnp.where(incoming, lengths[partner][source_slot], own_length)
        tables_two = jnp.where(incoming[:, None, None, None], adapters[partner][adapter_ids[partner][source_slot]], own_tables)
        fresh_two = fresh_second[index]
        keys_more = jnp.stack([fresh_prior[:, 0], fresh_two[:, 0]], 1)
        values_more = jnp.stack([fresh_prior[:, 1], fresh_two[:, 1]], 1)
        more_visible = jnp.stack([jnp.logical_not(vacated), jnp.ones((SLOTS,), bool)], 1)
        main_visible = (positions[None, :] < prior_length[:, None]) & jnp.logical_not(vacated)[:, None]
        queries_two = query_section(query_second[index], hidden_second[index], tables_two)
        attended_two = attend(queries_two, store_two[:, 0], store_two[:, 1], main_visible, keys_more, values_more, more_visible)
        update_two = output_section(attended_two, tables_two)
        return (attended_one, update_one, attended_two, update_two)
    results = lax.map(per_instance, jnp.arange(N_INST, dtype=jnp.int32))
    return (results[0], results[1], results[2], results[3])
```

```python
import math

import jax
import jax.numpy as jnp
from jax import lax
from jax.experimental import pallas as pl
from jax.experimental.pallas import tpu as pltpu
from jax.sharding import PartitionSpec as P

HEAD = 128
masked_score = -1e30
f32 = jnp.float32
bf16 = jnp.bfloat16


def dot_t(a, b):
    return lax.dot_general(a, b, (((1,), (1,)), ((), ())), preferred_element_type=f32)


def dot(a, b):
    return lax.dot_general(a, b, (((1,), (0,)), ((), ())), preferred_element_type=f32)


def twice(table):
    flat = table.reshape(-1, table.shape[-1])
    return jnp.concatenate([flat, flat], 0)


def row_iota(shape):
    return lax.broadcasted_iota(jnp.int32, shape, 0)


def lane_iota(shape):
    return lax.broadcasted_iota(jnp.int32, shape, 1)


def own_adapter(ids, me, slots, lanes, rank):
    rows, columns = row_iota((slots, lanes)), lane_iota((slots, lanes))
    adapter = jnp.zeros((slots, lanes), jnp.int32)
    for s in range(slots):
        adapter = jnp.where(rows == s, ids[me, s], adapter)
    return lax.rem(columns, lanes // 2) // rank == adapter


def moved_in(base, rows_at, counts, targets, sources, me, other):
    row = row_iota(base.shape)
    for m in range(targets.shape[1]):
        picked = rows_at[pl.ds(sources[other, m], 1), :]
        live = m < counts[other]
        base = jnp.where((row == targets[other, m]) & live, picked, base)
    return base


def is_row(shape, counts, table, instance):
    row = row_iota(shape)
    found = jnp.zeros(shape, jnp.bool_)
    for m in range(table.shape[1]):
        found = found | ((row == table[instance, m]) & (m < counts[instance]))
    return found


def rank_kernel(ids, counts, leave, land, h1, h2, h2_other, down, out, scratch):
    me = lax.axis_index("inst")
    peers, slots, lanes = out.shape
    rank = down.shape[2]
    table = twice(down[:, 0])
    first = dot_t(h1[...], table)
    second = dot_t(h2[...], table)
    scratch[...] = dot_t(h2_other[...], table)
    second = moved_in(second, scratch, counts, leave, land, me, me)
    both = jnp.where(lane_iota((slots, lanes)) < lanes // 2, first, second)
    both = jnp.where(own_adapter(ids, me, slots, lanes, rank), both, 0.0)
    for peer in range(peers):
        out[peer] = both


def attention_kernel(
    lengths, ids, counts, leave, land,
    ranks, base1, pack_own, pack_other, fresh1, up, down, cache,
    attn1_out, attn2_out, send_out, ranks_out,
    kv, other_rows, queries, mixed, second_rows, rank_rows, sems,
):
    me = lax.axis_index("inst")
    half = lax.axis_size("inst") // 2
    slots, width = base1.shape
    heads = width // HEAD
    cached = cache.shape[2]
    lanes = ranks.shape[2]
    rank = up.shape[2]
    copies = [pltpu.make_async_copy(cache.at[s], kv.at[s], sems.at[s]) for s in range(slots)]
    for copy in copies:
        copy.start()

    lane = lane_iota((slots, lanes))
    low = lane < lanes // 2
    total = ranks[0]
    for peer in range(1, ranks.shape[0]):
        total = total + ranks[peer]
    total = jnp.concatenate([jnp.where(low, total, 0.0), jnp.where(low, 0.0, total)], 0).astype(bf16)
    update = dot(total, twice(up[:, 0]))
    other_rows[...] = pack_other[...].astype(f32)
    own = pack_own[...].astype(f32)
    second = moved_in(own, other_rows, counts, leave, land, me, me)
    query1 = (base1[...].astype(f32) + update[:slots]).astype(bf16).astype(f32)
    query2 = (second[:, :width] + update[slots:]).astype(bf16).astype(f32)
    for h in range(heads):
        columns = slice(h * HEAD, (h + 1) * HEAD)
        queries[h, :slots] = query1[:, columns]
        queries[h, slots:] = query2[:, columns]
    key1 = fresh1[:, :HEAD].astype(f32)
    value1 = fresh1[:, HEAD:].astype(f32)
    key2 = second[:, width : width + HEAD]
    value2 = second[:, width + HEAD :]

    scaling = 1.0 / math.sqrt(HEAD)
    score_shape = (2 * heads, cached)
    position = lane_iota(score_shape)
    extra = (position == cached - 2) | ((position == cached - 1) & (row_iota(score_shape) >= heads))
    last = pl.ds(cached - 16, 16)
    tail_row = row_iota((16, HEAD))

    def with_fresh(tile, one, two):
        tile = jnp.where(tail_row == 14, one, tile.astype(f32))
        return jnp.where(tail_row == 15, two, tile).astype(bf16)

    for s in range(slots):
        copies[s].wait()
        row = slice(s, s + 1)
        kv[s, 0, last, :] = with_fresh(kv[s, 0, last, :], key1[row], key2[row])
        kv[s, 1, last, :] = with_fresh(kv[s, 1, last, :], value1[row], value2[row])
        query = jnp.concatenate([queries[:, s, :], queries[:, slots + s, :]], 0).astype(bf16)
        scores = dot_t(query, kv[s, 0]) * scaling
        scores = jnp.where((position < lengths[me, s]) | extra, scores, masked_score)
        weights = jnp.exp(scores - jnp.max(scores, 1, keepdims=True))
        probs = (weights / jnp.sum(weights, 1, keepdims=True)).astype(bf16)
        attended = dot(probs, kv[s, 1]).astype(bf16).astype(f32)
        mixed[0, s] = attended[:heads]
        mixed[1, s] = attended[heads:]

    vacated = is_row((slots, HEAD), counts, leave, me)
    fresh_value = own[:, width + HEAD :]
    for h in range(heads):
        columns = slice(h * HEAD, (h + 1) * HEAD)
        attn1_out[:, columns] = mixed[0, :, h, :].astype(bf16)
        served = mixed[1, :, h, :]
        second_rows[:, columns] = served
        attn2_out[:, columns] = jnp.where(vacated, fresh_value, served).astype(bf16)

    table = twice(down[:, 0])
    mask = own_adapter(ids, me, slots, lanes, rank)
    rank1 = jnp.where(mask, dot_t(attn1_out[...], table), 0.0)
    rank2 = jnp.where(mask, dot_t(attn2_out[...], table), 0.0)
    served_rows = second_rows[...]
    rank_rows[...] = jnp.where(mask, dot_t(served_rows.astype(bf16), table), 0.0)
    send_out[...] = moved_in(served_rows, second_rows, counts, land, leave, me, me).astype(bf16)
    for_own = jnp.where(low, rank1, rank2)
    for_other = moved_in(jnp.zeros_like(for_own), rank_rows, counts, land, leave, me, me)
    peers = ranks_out.shape[0] // 2
    lower = me < half
    for peer in range(peers):
        ranks_out[peer] = jnp.where(lower, for_own, for_other)
        ranks_out[peers + peer] = jnp.where(lower, for_other, for_own)


def delta_kernel(counts, land, ranks, up, up_other, attn2_own, attn2_other, delta1_out, delta2_out, attn2_out):
    me = lax.axis_index("inst")
    half = lax.axis_size("inst") // 2
    other = jnp.bitwise_xor(me, half)
    peers = ranks.shape[0] // 2
    _, slots, lanes = ranks.shape
    sums = []
    for part in range(2):
        total = ranks[part * peers]
        for peer in range(1, peers):
            total = total + ranks[part * peers + peer]
        sums.append(total)
    lower = me < half
    own = jnp.where(lower, sums[0], sums[1])
    got = jnp.where(lower, sums[1], sums[0])
    low = lane_iota((slots, lanes)) < lanes // 2
    incoming = is_row((slots, lanes), counts, land, other)
    rank1 = jnp.where(low, own, 0.0)
    rank2 = jnp.where(low, pltpu.roll(own, lanes // 2, 1), got)
    rank2 = jnp.where(incoming == low, 0.0, rank2)
    table = jnp.concatenate([up[:, 0].reshape(-1, up.shape[3]), up_other[...]], 0)
    delta = dot(jnp.concatenate([rank1, rank2], 0).astype(bf16), table).astype(bf16)
    delta1_out[...] = delta[:slots]
    delta2_out[...] = delta[slots:]
    incoming = is_row(attn2_out.shape, counts, land, other)
    attn2_out[...] = jnp.where(incoming, attn2_other[...].astype(f32), attn2_own[...].astype(f32)).astype(bf16)


def per_device(
    query_first,
    query_second,
    hidden_first,
    hidden_second,
    fresh_first,
    fresh_second,
    kv_cache,
    adapters,
    lengths,
    adapter_ids,
    move_counts,
    move_from,
    move_to,
):
    inst_count = lax.axis_size("inst")
    peers = lax.axis_size("tensor")
    half = inst_count // 2
    swap = [(i, i ^ half) for i in range(inst_count)]
    groups = [
        [i * peers + t for t in range(peers)] + [(i + half) * peers + t for t in range(peers)] for i in range(half)
    ]
    _, slots, width = query_first.shape
    tables = adapters[0]
    pool, _, rank, _ = tables.shape
    lanes = 2 * pool * rank
    heads = width // HEAD
    cached = kv_cache.shape[3]

    smem = pl.BlockSpec(memory_space=pltpu.SMEM)
    vmem = pl.BlockSpec(memory_space=pltpu.VMEM)
    anywhere = pl.BlockSpec(memory_space=pl.ANY)

    def part(which):
        return pl.BlockSpec((pool, 1, rank, width), lambda step: (0, which, 0, 0))

    def shape(dims, dtype):
        return jax.ShapeDtypeStruct(dims, dtype)

    hidden_other = lax.ppermute(hidden_second[0], "inst", swap)
    pack_own = jnp.concatenate([query_second[0], fresh_second[0].reshape(slots, 2 * HEAD)], 1)
    pack_other = lax.ppermute(pack_own, "inst", swap)
    fresh1 = fresh_first[0].reshape(slots, 2 * HEAD)

    ranks = pl.pallas_call(
        rank_kernel,
        name="rank_partials",
        grid=(1,),
        out_shape=shape((peers, slots, lanes), f32),
        in_specs=[smem] * 4 + [vmem] * 3 + [part(0)],
        out_specs=vmem,
        scratch_shapes=[pltpu.VMEM((slots, lanes), f32)],
    )(adapter_ids, move_counts, move_from, move_to, hidden_first[0], hidden_second[0], hidden_other, tables)
    ranks = lax.all_to_all(ranks, "tensor", 0, 0)

    up_other = lax.ppermute(tables[:, 3].reshape(pool * rank, width), "inst", swap)

    attn1, attn2_own, attn2_send, ranks_two = pl.pallas_call(
        attention_kernel,
        name="attention",
        grid=(1,),
        out_shape=(
            shape((slots, width), bf16),
            shape((slots, width), bf16),
            shape((slots, width), bf16),
            shape((2 * peers, slots, lanes), f32),
        ),
        in_specs=[smem] * 5 + [vmem] * 5 + [part(1), part(2), anywhere],
        out_specs=(vmem,) * 4,
        scratch_shapes=[
            pltpu.VMEM((slots, 2, cached, HEAD), bf16),
            pltpu.VMEM((slots, width + 2 * HEAD), f32),
            pltpu.VMEM((heads, 2 * slots, HEAD), f32),
            pltpu.VMEM((2, slots, heads, HEAD), f32),
            pltpu.VMEM((slots, width), f32),
            pltpu.VMEM((slots, lanes), f32),
            pltpu.SemaphoreType.DMA((slots,)),
        ],
        compiler_params=pltpu.CompilerParams(vmem_limit_bytes=16 * 1024 * 1024),
    )(
        lengths, adapter_ids, move_counts, move_from, move_to,
        ranks, query_first[0], pack_own, pack_other, fresh1, tables, tables, kv_cache[0],
    )
    ranks_two = lax.all_to_all(ranks_two, ("inst", "tensor"), 0, 0, axis_index_groups=groups)
    attn2_other = lax.ppermute(attn2_send, "inst", swap)

    delta1, delta2, attn2 = pl.pallas_call(
        delta_kernel,
        name="deltas",
        grid=(1,),
        out_shape=(shape((slots, width), bf16),) * 3,
        in_specs=[smem] * 2 + [vmem, part(3)] + [vmem] * 3,
        out_specs=(vmem,) * 3,
    )(move_counts, move_to, ranks_two, tables, up_other, attn2_own, attn2_other)
    return (attn1[None], delta1[None], attn2[None], delta2[None])


def solution(mesh):
    row = P("inst", None, "tensor")
    fresh = P("inst", None, None, "tensor")
    whole = P("inst", None, None, None, "tensor")
    return jax.shard_map(
        per_device,
        mesh=mesh,
        in_specs=(row, row, row, row, fresh, fresh, whole, whole, P(), P(), P(), P(), P()),
        out_specs=(row, row, row, row),
        check_vma=False,
    )
```

```python
import math

import jax
import jax.numpy as jnp
from jax import lax
from jax.experimental import pallas as pl
from jax.experimental.pallas import tpu as pltpu
from jax.sharding import PartitionSpec as P

HEAD = 128
masked_score = -1e30
f32 = jnp.float32
bf16 = jnp.bfloat16


def dot_t(a, b):
    return lax.dot_general(a, b, (((1,), (1,)), ((), ())), preferred_element_type=f32)


def dot(a, b):
    return lax.dot_general(a, b, (((1,), (0,)), ((), ())), preferred_element_type=f32)


def twice(table):
    flat = table.reshape(-1, table.shape[-1])
    return jnp.concatenate([flat, flat], 0)


def row_iota(shape):
    return lax.broadcasted_iota(jnp.int32, shape, 0)


def lane_iota(shape):
    return lax.broadcasted_iota(jnp.int32, shape, 1)


def own_adapter(ids, me, slots, lanes, rank):
    rows, columns = row_iota((slots, lanes)), lane_iota((slots, lanes))
    adapter = jnp.zeros((slots, lanes), jnp.int32)
    for s in range(slots):
        adapter = jnp.where(rows == s, ids[s, me], adapter)
    return lax.rem(columns, lanes // 2) // rank == adapter


def moved_in(base, rows_at, counts, targets, sources, me):
    row = row_iota(base.shape)
    for m in range(targets.shape[0]):
        picked = rows_at[pl.ds(sources[m, me], 1), :]
        base = jnp.where((row == targets[m, me]) & (m < counts[me]), picked, base)
    return base


def is_row(shape, counts, table, instance):
    row = row_iota(shape)
    found = jnp.zeros(shape, jnp.bool_)
    for m in range(table.shape[0]):
        found = found | ((row == table[m, instance]) & (m < counts[instance]))
    return found


def start_all(pairs, sems, first=0):
    copies = [pltpu.make_async_copy(src, dst, sems.at[first + n]) for n, (src, dst) in enumerate(pairs)]
    for copy in copies:
        copy.start()
    return copies


def wait_all(copies):
    for copy in copies:
        copy.wait()


def rank_kernel(
    ids_at, counts_at, leave_at, land_at, h1_at, h2_at, query_at, fresh_at, tables_at, h2_other,
    out, pack_out,
    ids, counts, leave, land, h1, h2, query, fresh, down, fresh_wide, scratch, sems,
):
    me = lax.axis_index("inst")
    copies = start_all(
        [
            (h1_at.at[0], h1), (h2_at.at[0], h2), (tables_at.at[0, :, 0], down), (ids_at, ids), (counts_at, counts),
            (leave_at, leave), (land_at, land), (query_at.at[0], query), (fresh_at.at[0], fresh),
        ],
        sems,
    )
    peers, slots, lanes = out.shape
    width = h1.shape[1]
    rank = down.shape[1]
    wait_all(copies)
    table = twice(down[...])
    hidden = jnp.concatenate([h1[...].astype(f32), h2[...].astype(f32), h2_other[...].astype(f32)], 0).astype(bf16)
    partials = dot_t(hidden, table)
    scratch[...] = partials[2 * slots :]
    second = moved_in(partials[slots : 2 * slots], scratch, counts, leave, land, me)
    both = jnp.where(lane_iota((slots, lanes)) < lanes // 2, partials[:slots], second)
    both = jnp.where(own_adapter(ids, me, slots, lanes, rank), both, 0.0)
    for peer in range(peers):
        out[peer] = both
    pack_out[:, :width] = query[...]
    fresh_wide[...] = fresh[...].astype(f32)
    pack_out[:, width : width + HEAD] = fresh_wide[:, 0, :].astype(bf16)
    pack_out[:, width + HEAD :] = fresh_wide[:, 1, :].astype(bf16)


def attention_kernel(
    lengths_at, ids_at, counts_at, leave_at, land_at, base1_at, fresh1_at, tables_at, cache_at,
    ranks, pack_own, pack_other,
    attn1_out, attn2_out, send_out, ranks_out, up_out, incoming_out,
    lengths, ids, counts, leave, land, base1, fresh1, up, down,
    kv, other_rows, queries, scores, mixed, second_rows, rank_rows, sems,
):
    me = lax.axis_index("inst")
    half = lax.axis_size("inst") // 2
    other = jnp.bitwise_xor(me, half)
    slots, width = base1.shape
    heads = width // HEAD
    cached = kv.shape[2]
    lanes = ranks.shape[2]
    rank = up.shape[1]
    small = start_all(
        [
            (tables_at.at[0, :, 1], up), (base1_at.at[0], base1), (lengths_at, lengths), (ids_at, ids),
            (counts_at, counts), (leave_at, leave), (land_at, land), (fresh1_at.at[0], fresh1),
        ],
        sems,
    )
    keys = start_all([(cache_at.at[0, s, 0], kv.at[0, s]) for s in range(slots)], sems, 8)
    values = start_all([(cache_at.at[0, s, 1], kv.at[1, s]) for s in range(slots)], sems, 8 + slots)
    late = start_all(
        [(tables_at.at[0, :, 2], down), (tables_at.at[0, :, 3], up_out)], sems, 8 + 2 * slots
    )

    lane = lane_iota((slots, lanes))
    low = lane < lanes // 2
    total = ranks[0]
    for peer in range(1, ranks.shape[0]):
        total = total + ranks[peer]
    total = jnp.concatenate([jnp.where(low, total, 0.0), jnp.where(low, 0.0, total)], 0).astype(bf16)
    other_rows[...] = pack_other[...].astype(f32)
    own = pack_own[...].astype(f32)
    wait_all(small)
    update = dot(total, twice(up[...]))
    second = moved_in(own, other_rows, counts, leave, land, me)
    query1 = (base1[...].astype(f32) + update[:slots]).astype(bf16).astype(f32)
    query2 = (second[:, :width] + update[slots:]).astype(bf16).astype(f32)
    for h in range(heads):
        columns = slice(h * HEAD, (h + 1) * HEAD)
        queries[h, :slots] = query1[:, columns]
        queries[h, slots:] = query2[:, columns]
    first = fresh1[...].astype(f32)
    key2 = second[:, width : width + HEAD]
    value2 = second[:, width + HEAD :]

    scaling = math.log2(math.e) / math.sqrt(HEAD)
    score_shape = (2 * heads, cached)
    position = lane_iota(score_shape)
    extra = (position == cached - 2) | ((position == cached - 1) & (row_iota(score_shape) >= heads))
    last = pl.ds(cached - 16, 16)
    tail_row = row_iota((16, HEAD))

    def with_fresh(tile, one, two):
        tile = jnp.where(tail_row == 14, one, tile.astype(f32))
        return jnp.where(tail_row == 15, two, tile).astype(bf16)

    step = 2
    for block in range(0, slots, step):
        wait_all(keys[block : block + step])
        for s in range(block, block + step):
            kv[0, s, last, :] = with_fresh(kv[0, s, last, :], first[s, 0:1], key2[s : s + 1])
            query = jnp.concatenate([queries[:, s, :], queries[:, slots + s, :]], 0).astype(bf16)
            score = dot_t(query, kv[0, s]) * scaling
            scores[s] = jnp.where((position < lengths[s, me]) | extra, score, masked_score)
    for block in range(0, slots, step):
        wait_all(values[block : block + step])
        for s in range(block, block + step):
            kv[1, s, last, :] = with_fresh(kv[1, s, last, :], first[s, 1:2], value2[s : s + 1])
            score = scores[s]
            weights = jnp.exp2(score - jnp.max(score, 1, keepdims=True))
            probs = (weights * (1.0 / jnp.sum(weights, 1, keepdims=True))).astype(bf16)
            attended = dot(probs, kv[1, s]).astype(bf16).astype(f32)
            mixed[0, s] = attended[:heads]
            mixed[1, s] = attended[heads:]

    vacated = is_row((slots, HEAD), counts, leave, me)
    fresh_value = own[:, width + HEAD :]
    for h in range(heads):
        columns = slice(h * HEAD, (h + 1) * HEAD)
        attn1_out[:, columns] = mixed[0, :, h, :].astype(bf16)
        served = mixed[1, :, h, :]
        second_rows[:, columns] = served
        attn2_out[:, columns] = jnp.where(vacated, fresh_value, served).astype(bf16)

    wait_all(late)
    mask = own_adapter(ids, me, slots, lanes, rank)
    served_rows = second_rows[...]
    stacked = jnp.concatenate([attn1_out[...].astype(f32), attn2_out[...].astype(f32), served_rows], 0).astype(bf16)
    partials = dot_t(stacked, twice(down[...]))
    rank_rows[...] = jnp.where(mask, partials[2 * slots :], 0.0)
    send_out[...] = moved_in(served_rows, second_rows, counts, land, leave, me).astype(bf16)
    for_own = jnp.where(mask, jnp.where(low, partials[:slots], partials[slots : 2 * slots]), 0.0)
    for_other = moved_in(jnp.zeros_like(for_own), rank_rows, counts, land, leave, me)
    peers = ranks_out.shape[0] // 2
    lower = me < half
    for peer in range(peers):
        ranks_out[peer] = jnp.where(lower, for_own, for_other)
        ranks_out[peers + peer] = jnp.where(lower, for_other, for_own)
    incoming_out[...] = jnp.where(is_row(incoming_out.shape, counts, land, other), 1.0, 0.0)


def delta_kernel(ranks, up, up_other, attn2_own, attn2_other, incoming, delta1_out, delta2_out, attn2_out):
    lower = lax.axis_index("inst") < lax.axis_size("inst") // 2
    peers = ranks.shape[0] // 2
    _, slots, lanes = ranks.shape
    sums = []
    for part in range(2):
        total = ranks[part * peers]
        for peer in range(1, peers):
            total = total + ranks[part * peers + peer]
        sums.append(total)
    own = jnp.where(lower, sums[0], sums[1])
    got = jnp.where(lower, sums[1], sums[0])
    low = lane_iota((slots, lanes)) < lanes // 2
    comes = incoming[...] > 0.5
    rank1 = jnp.where(low, own, 0.0)
    rank2_own = jnp.where(low, pltpu.roll(own, lanes // 2, 1), 0.0)
    rank2_got = jnp.where(low, 0.0, got)
    rank2 = jnp.where(comes, rank2_got, rank2_own)
    table = jnp.concatenate([up[...].reshape(-1, up.shape[2]), up_other[...]], 0)
    delta = dot(jnp.concatenate([rank1, rank2], 0).astype(bf16), table)
    delta1_out[...] = delta[:slots].astype(bf16)
    delta2_out[...] = delta[slots:].astype(bf16)
    for first in range(0, attn2_out.shape[1], lanes):
        columns = slice(first, first + lanes)
        attn2_out[:, columns] = jnp.where(
            comes, attn2_other[:, columns].astype(f32), attn2_own[:, columns].astype(f32)
        ).astype(bf16)


def per_device(
    query_first,
    query_second,
    hidden_first,
    hidden_second,
    fresh_first,
    fresh_second,
    kv_cache,
    adapters,
    lengths,
    adapter_ids,
    move_counts,
    move_from,
    move_to,
):
    inst_count = lax.axis_size("inst")
    peers = lax.axis_size("tensor")
    half = inst_count // 2
    swap = [(i, i ^ half) for i in range(inst_count)]
    groups = [
        [i * peers + t for t in range(peers)] + [(i + half) * peers + t for t in range(peers)] for i in range(half)
    ]
    _, slots, width = query_first.shape
    _, pool, _, rank, _ = adapters.shape
    moves = move_from.shape[1]
    lanes = 2 * pool * rank
    heads = width // HEAD
    cached = kv_cache.shape[3]
    lengths, adapter_ids, move_from, move_to = lengths.T, adapter_ids.T, move_from.T, move_to.T

    hbm = pl.BlockSpec(memory_space=pltpu.HBM)
    vmem = pl.BlockSpec(memory_space=pltpu.VMEM)

    def shape(dims, dtype):
        return jax.ShapeDtypeStruct(dims, dtype)

    def far(*arrays):
        return [pltpu.with_memory_space_constraint(array, pltpu.HBM) for array in arrays]

    def near(*arrays):
        return [pltpu.with_memory_space_constraint(array, pltpu.VMEM) for array in arrays]

    def near_shape(dims, dtype):
        return pltpu.VMEM(dims, dtype)

    table = pltpu.VMEM((pool, rank, width), bf16)
    rows = pltpu.VMEM((slots, width), bf16)
    fresh = pltpu.VMEM((slots, 2, HEAD), bf16)
    by_slot = pltpu.SMEM((slots, inst_count), jnp.int32)
    by_inst = pltpu.SMEM((inst_count,), jnp.int32)
    by_move = pltpu.SMEM((moves, inst_count), jnp.int32)

    hidden_other = lax.ppermute(hidden_second[0], "inst", swap)
    up_other = lax.ppermute(adapters[0, :, 3].reshape(pool * rank, width), "inst", swap)

    ranks, pack_own = pl.pallas_call(
        rank_kernel,
        name="rank_partials",
        out_shape=(shape((peers, slots, lanes), f32), shape((slots, width + 2 * HEAD), bf16)),
        in_specs=[hbm] * 9 + [vmem],
        out_specs=(vmem,) * 2,
        scratch_shapes=[
            by_slot, by_inst, by_move, by_move, rows, rows, rows, fresh, table,
            pltpu.VMEM((slots, 2, HEAD), f32),
            pltpu.VMEM((slots, lanes), f32),
            pltpu.SemaphoreType.DMA((9,)),
        ],
        compiler_params=pltpu.CompilerParams(vmem_limit_bytes=16 * 1024 * 1024),
    )(
        *far(
            adapter_ids, move_counts, move_from, move_to,
            hidden_first, hidden_second, query_second, fresh_second, adapters,
        ),
        *near(hidden_other),
    )
    ranks = lax.all_to_all(ranks, "tensor", 0, 0)
    pack_other = lax.ppermute(pack_own, "inst", swap)

    attn1, attn2_own, attn2_send, ranks_two, up_own, incoming = pl.pallas_call(
        attention_kernel,
        name="attention",
        out_shape=(
            shape((slots, width), bf16),
            shape((slots, width), bf16),
            shape((slots, width), bf16),
            shape((2 * peers, slots, lanes), f32),
            shape((pool, rank, width), bf16),
            shape((slots, lanes), f32),
        ),
        in_specs=[hbm] * 9 + [vmem] * 3,
        out_specs=(vmem,) * 6,
        scratch_shapes=[
            by_slot, by_slot, by_inst, by_move, by_move, rows, fresh, table, table,
            pltpu.VMEM((2, slots, cached, HEAD), bf16),
            pltpu.VMEM((slots, width + 2 * HEAD), f32),
            pltpu.VMEM((heads, 2 * slots, HEAD), f32),
            pltpu.VMEM((slots, 2 * heads, cached), f32),
            pltpu.VMEM((2, slots, heads, HEAD), f32),
            pltpu.VMEM((slots, width), f32),
            pltpu.VMEM((slots, lanes), f32),
            pltpu.SemaphoreType.DMA((10 + 2 * slots,)),
        ],
        compiler_params=pltpu.CompilerParams(vmem_limit_bytes=16 * 1024 * 1024),
    )(
        *far(lengths, adapter_ids, move_counts, move_from, move_to, query_first, fresh_first, adapters, kv_cache),
        *near(ranks, pack_own, pack_other),
    )
    ranks_two = lax.all_to_all(ranks_two, ("inst", "tensor"), 0, 0, axis_index_groups=groups)
    attn2_other = lax.ppermute(attn2_send, "inst", swap)

    delta1, delta2, attn2 = pl.pallas_call(
        delta_kernel,
        name="deltas",
        out_shape=(shape((slots, width), bf16),) * 3,
        in_specs=[vmem] * 6,
        out_specs=(vmem,) * 3,
        compiler_params=pltpu.CompilerParams(vmem_limit_bytes=16 * 1024 * 1024),
    )(*near(ranks_two, up_own, up_other, attn2_own, attn2_other, incoming))
    return (attn1[None], delta1[None], attn2[None], delta2[None])


def solution(mesh):
    row = P("inst", None, "tensor")
    fresh = P("inst", None, None, "tensor")
    whole = P("inst", None, None, None, "tensor")
    return jax.shard_map(
        per_device,
        mesh=mesh,
        in_specs=(row, row, row, row, fresh, fresh, whole, whole, P(), P(), P(), P(), P()),
        out_specs=(row, row, row, row),
        check_vma=False,
    )
```

```python
import math

import jax
import jax.numpy as jnp
from jax import lax
from jax.experimental import pallas as pl
from jax.experimental.pallas import tpu as pltpu
from jax.sharding import PartitionSpec as P

HEAD = 128
masked_score = -1e30
f32 = jnp.float32
bf16 = jnp.bfloat16


def dot_t(a, b):
    return lax.dot_general(a, b, (((1,), (1,)), ((), ())), preferred_element_type=f32)


def dot(a, b):
    return lax.dot_general(a, b, (((1,), (0,)), ((), ())), preferred_element_type=f32)


def twice(table):
    flat = table.reshape(-1, table.shape[-1])
    return jnp.concatenate([flat, flat], 0)


def row_iota(shape):
    return lax.broadcasted_iota(jnp.int32, shape, 0)


def lane_iota(shape):
    return lax.broadcasted_iota(jnp.int32, shape, 1)


def own_adapter(ids, me, slots, lanes, rank):
    rows, columns = row_iota((slots, lanes)), lane_iota((slots, lanes))
    adapter = jnp.zeros((slots, lanes), jnp.int32)
    for s in range(slots):
        adapter = jnp.where(rows == s, ids[s, me], adapter)
    return lax.rem(columns, lanes // 2) // rank == adapter


def moved_in(base, rows_at, counts, targets, sources, me):
    row = row_iota(base.shape)
    for m in range(targets.shape[0]):
        picked = rows_at[pl.ds(sources[m, me], 1), :]
        base = jnp.where((row == targets[m, me]) & (m < counts[me]), picked, base)
    return base


def is_row(shape, counts, table, instance):
    row = row_iota(shape)
    found = jnp.zeros(shape, jnp.bool_)
    for m in range(table.shape[0]):
        found = found | ((row == table[m, instance]) & (m < counts[instance]))
    return found


def start_all(pairs, sems, first=0):
    copies = [pltpu.make_async_copy(src, dst, sems.at[first + n]) for n, (src, dst) in enumerate(pairs)]
    for copy in copies:
        copy.start()
    return copies


def wait_all(copies):
    for copy in copies:
        copy.wait()


def halves(value):
    high = value.astype(bf16).astype(f32)
    return jnp.concatenate([high, value - high], 0)


def stage_kernel(
    h1, h2, q1, q2, f1, f2, tables_at,
    first_out, second_out, tables_out, up_out,
    fresh, fresh_wide, sems,
):
    width = h1.shape[2]
    copies = start_all(
        [
            (f1.at[0], fresh.at[0]), (f2.at[0], fresh.at[1]),
            (h1.at[0], first_out.at[:, :width]), (h2.at[0], second_out.at[:, :width]),
            (q1.at[0], first_out.at[:, width : 2 * width]), (q2.at[0], second_out.at[:, width : 2 * width]),
            (tables_at.at[0, :, 3], up_out), (tables_at.at[0], tables_out),
        ],
        sems,
    )
    wait_all(copies[:2])
    fresh_wide[...] = fresh[...].astype(f32)
    for step, out in enumerate((first_out, second_out)):
        out[:, 2 * width : 2 * width + HEAD] = fresh_wide[step, :, 0, :].astype(bf16)
        out[:, 2 * width + HEAD :] = fresh_wide[step, :, 1, :].astype(bf16)
    wait_all(copies[2:])


def rank_kernel(
    ids_at, counts_at, leave_at, land_at, first, second, other, tables,
    out,
    ids, counts, leave, land, scratch, sems,
):
    me = lax.axis_index("inst")
    copies = start_all([(ids_at, ids), (counts_at, counts), (leave_at, leave), (land_at, land)], sems)
    peers, _, lanes = out.shape
    slots = first.shape[0]
    width = tables.shape[3]
    rank = tables.shape[2]
    table = twice(tables[:, 0])
    hidden = [ref[:, :width].astype(f32) for ref in (first, second, other)]
    partials = dot_t(jnp.concatenate(hidden, 0).astype(bf16), table)
    scratch[...] = partials[2 * slots :]
    wait_all(copies)
    moved = moved_in(partials[slots : 2 * slots], scratch, counts, leave, land, me)
    both = jnp.where(lane_iota((slots, lanes)) < lanes // 2, partials[:slots], moved)
    both = jnp.where(own_adapter(ids, me, slots, lanes, rank), both, 0.0)
    for peer in range(peers):
        out[peer] = both


def attention_kernel(
    lengths_at, ids_at, counts_at, leave_at, land_at, cache_at,
    ranks, first_rows, second_rows, got_rows, tables, up_other,
    attn1_out, own_out, landing_out, sums_out,
    lengths, ids, counts, leave, land,
    kv, other_rows, queries, scores, mixed, served_rows, rank_rows, sems,
):
    me = lax.axis_index("inst")
    half = lax.axis_size("inst") // 2
    slots, width = attn1_out.shape
    heads = width // HEAD
    cached = kv.shape[2]
    lanes = ranks.shape[2]
    rank = tables.shape[2]
    moves = leave.shape[0]
    small = start_all(
        [(counts_at, counts), (leave_at, leave), (land_at, land), (lengths_at, lengths), (ids_at, ids)], sems
    )
    keys = start_all([(cache_at.at[0, s, 0], kv.at[0, s]) for s in range(slots)], sems, 5)
    values = start_all([(cache_at.at[0, s, 1], kv.at[1, s]) for s in range(slots)], sems, 5 + slots)

    lane = lane_iota((slots, lanes))
    low = lane < lanes // 2
    total = ranks[0]
    for peer in range(1, ranks.shape[0]):
        total = total + ranks[peer]
    total = jnp.concatenate([jnp.where(low, total, 0.0), jnp.where(low, 0.0, total)], 0).astype(bf16)
    update = dot(total, twice(tables[:, 1]))
    other_rows[...] = got_rows[:, width:].astype(f32)
    first = first_rows[:, width:].astype(f32)
    own = second_rows[:, width:].astype(f32)
    wait_all(small)
    second = moved_in(own, other_rows, counts, leave, land, me)
    query1 = (first[:, :width] + update[:slots]).astype(bf16).astype(f32)
    query2 = (second[:, :width] + update[slots:]).astype(bf16).astype(f32)
    for h in range(heads):
        columns = slice(h * HEAD, (h + 1) * HEAD)
        queries[h, :slots] = query1[:, columns]
        queries[h, slots:] = query2[:, columns]
    key1, value1 = first[:, width : width + HEAD], first[:, width + HEAD :]
    key2, value2 = second[:, width : width + HEAD], second[:, width + HEAD :]

    scaling = math.log2(math.e) / math.sqrt(HEAD)
    score_shape = (2 * heads, cached)
    position = lane_iota(score_shape)
    extra = (position == cached - 2) | ((position == cached - 1) & (row_iota(score_shape) >= heads))
    last = pl.ds(cached - 16, 16)
    tail_row = row_iota((16, HEAD))

    def with_fresh(tile, one, two):
        tile = jnp.where(tail_row == 14, one, tile.astype(f32))
        return jnp.where(tail_row == 15, two, tile).astype(bf16)

    step = 2
    for block in range(0, slots, step):
        wait_all(keys[block : block + step])
        for s in range(block, block + step):
            kv[0, s, last, :] = with_fresh(kv[0, s, last, :], key1[s : s + 1], key2[s : s + 1])
            query = jnp.concatenate([queries[:, s, :], queries[:, slots + s, :]], 0).astype(bf16)
            score = dot_t(query, kv[0, s]) * scaling
            scores[s] = jnp.where((position < lengths[s, me]) | extra, score, masked_score)
    for block in range(0, slots, step):
        wait_all(values[block : block + step])
        for s in range(block, block + step):
            kv[1, s, last, :] = with_fresh(kv[1, s, last, :], value1[s : s + 1], value2[s : s + 1])
            score = scores[s]
            weights = jnp.exp2(score - jnp.max(score, 1, keepdims=True))
            probs = (weights * (1.0 / jnp.sum(weights, 1, keepdims=True))).astype(bf16)
            attended = dot(probs, kv[1, s]).astype(bf16).astype(f32)
            mixed[s] = attended[:heads]
            mixed[slots + s] = attended[heads:]

    vacated = is_row((slots, HEAD), counts, leave, me)
    for h in range(heads):
        columns = slice(h * HEAD, (h + 1) * HEAD)
        served = mixed[slots:, h, :]
        served_rows[:slots, columns] = mixed[:slots, h, :]
        served_rows[slots : 2 * slots, columns] = jnp.where(vacated, own[:, width + HEAD :], served)
        served_rows[2 * slots :, columns] = served
    stacked = served_rows[...].astype(bf16)
    attn1_out[...] = served_rows[:slots].astype(bf16)
    own_out[...] = served_rows[slots : 2 * slots]

    partials = dot_t(stacked, twice(tables[:, 2]))
    mask = own_adapter(ids, me, slots, lanes, rank)
    rank_rows[...] = jnp.where(mask, partials[2 * slots :], 0.0)
    for_own = jnp.where(mask, jnp.where(low, partials[:slots], partials[slots : 2 * slots]), 0.0)
    for_other = moved_in(jnp.zeros_like(for_own), rank_rows, counts, land, leave, me)
    peers = sums_out.shape[0] // 2
    lower = me < half
    for_own, for_other = halves(for_own), halves(for_other)
    in_low = jnp.where(lower, for_own, for_other).astype(bf16)
    in_high = jnp.where(lower, for_other, for_own).astype(bf16)
    sent = jnp.concatenate([mixed[slots + leave[m, me]] for m in range(moves)], 0).astype(bf16)
    for peer in range(peers):
        sums_out[peer, : 2 * slots] = in_low
        sums_out[peers + peer, : 2 * slots] = in_high
        sums_out[peer, 2 * slots :] = sent
        sums_out[peers + peer, 2 * slots :] = sent
    other = jnp.bitwise_xor(me, half)
    row = row_iota((slots, lanes))
    for m in range(moves):
        lands = (row == land[m, other]) & (m < counts[other])
        landing_out[m] = jnp.where(lands, 1.0, 0.0)


def delta_kernel(sums, up, up_other, attn2_own, landing, delta1_out, delta2_out, attn2_out):
    lower = lax.axis_index("inst") < lax.axis_size("inst") // 2
    peers = sums.shape[0] // 2
    lanes = sums.shape[2]
    slots, width = attn2_out.shape
    heads = width // HEAD
    moves = landing.shape[0]
    totals = []
    for part in range(2):
        total = sums[part * peers, : 2 * slots].astype(f32)
        for peer in range(1, peers):
            total = total + sums[part * peers + peer, : 2 * slots].astype(f32)
        totals.append(total[:slots] + total[slots:])
    own = jnp.where(lower, totals[0], totals[1])
    got = jnp.where(lower, totals[1], totals[0])
    low = lane_iota((slots, lanes)) < lanes // 2
    rank1 = jnp.where(low, own, 0.0)
    rank2_own = jnp.where(low, pltpu.roll(own, lanes // 2, 1), 0.0)
    rank2_got = jnp.where(low, 0.0, got)
    lands = [landing[m] > 0.5 for m in range(moves)]
    rank2 = rank2_own
    for m in range(moves):
        rank2 = jnp.where(lands[m], rank2_got, rank2)
    table = jnp.concatenate([up[...], up_other[...]], 0)
    delta = dot(jnp.concatenate([rank1, rank2], 0).astype(bf16), table)
    delta1_out[...] = delta[:slots].astype(bf16)
    delta2_out[...] = delta[slots:].astype(bf16)
    sender = jnp.where(lower, peers, 0) + lax.axis_index("tensor")
    moved = sums[sender, 2 * slots :, :].astype(f32)
    for h in range(heads):
        columns = slice(h * HEAD, (h + 1) * HEAD)
        rows = attn2_own[:, columns]
        for m in range(moves):
            rows = jnp.where(lands[m], moved[m * heads + h : m * heads + h + 1], rows)
        attn2_out[:, columns] = rows.astype(bf16)


def per_device(
    query_first,
    query_second,
    hidden_first,
    hidden_second,
    fresh_first,
    fresh_second,
    kv_cache,
    adapters,
    lengths,
    adapter_ids,
    move_counts,
    move_from,
    move_to,
):
    inst_count = lax.axis_size("inst")
    peers = lax.axis_size("tensor")
    half = inst_count // 2
    swap = [(i, i ^ half) for i in range(inst_count)]
    groups = [
        [i * peers + t for t in range(peers)] + [(i + half) * peers + t for t in range(peers)] for i in range(half)
    ]
    _, slots, width = query_first.shape
    _, pool, _, rank, _ = adapters.shape
    moves = move_from.shape[1]
    lanes = 2 * pool * rank
    heads = width // HEAD
    cached = kv_cache.shape[3]
    lengths, adapter_ids, move_from, move_to = lengths.T, adapter_ids.T, move_from.T, move_to.T

    hbm = pl.BlockSpec(memory_space=pltpu.HBM)
    vmem = pl.BlockSpec(memory_space=pltpu.VMEM)
    params = pltpu.CompilerParams(vmem_limit_bytes=16 * 1024 * 1024)

    def shape(dims, dtype):
        return jax.ShapeDtypeStruct(dims, dtype)

    def far(*arrays):
        return [pltpu.with_memory_space_constraint(array, pltpu.HBM) for array in arrays]

    def near(*arrays):
        return [pltpu.with_memory_space_constraint(array, pltpu.VMEM) for array in arrays]

    by_slot = pltpu.SMEM((slots, inst_count), jnp.int32)
    by_inst = pltpu.SMEM((inst_count,), jnp.int32)
    by_move = pltpu.SMEM((moves, inst_count), jnp.int32)
    rows = shape((slots, 2 * width + 2 * HEAD), bf16)

    first, second, tables, up_own = pl.pallas_call(
        stage_kernel,
        name="stage",
        out_shape=(rows, rows, shape(adapters.shape[1:], bf16), shape((pool, rank, width), bf16)),
        in_specs=[hbm] * 7,
        out_specs=(vmem,) * 4,
        scratch_shapes=[
            pltpu.VMEM((2, slots, 2, HEAD), bf16),
            pltpu.VMEM((2, slots, 2, HEAD), f32),
            pltpu.SemaphoreType.DMA((8,)),
        ],
        compiler_params=params,
    )(*far(hidden_first, hidden_second, query_first, query_second, fresh_first, fresh_second, adapters))
    up_own = up_own.reshape(pool * rank, width)
    up_other = lax.ppermute(up_own, "inst", swap)
    other = lax.ppermute(second, "inst", swap)

    ranks = pl.pallas_call(
        rank_kernel,
        name="rank_partials",
        out_shape=shape((peers, slots, lanes), f32),
        in_specs=[hbm] * 4 + [vmem] * 4,
        out_specs=vmem,
        scratch_shapes=[
            by_slot, by_inst, by_move, by_move,
            pltpu.VMEM((slots, lanes), f32),
            pltpu.SemaphoreType.DMA((4,)),
        ],
        cost_estimate=pl.CostEstimate(flops=2 * 10**10, bytes_accessed=10**8, transcendentals=0),
        compiler_params=params,
    )(*far(adapter_ids, move_counts, move_from, move_to), *near(first, second, other, tables))
    ranks = lax.all_to_all(ranks, "tensor", 0, 0)

    attn1, attn2_own, landing, sums = pl.pallas_call(
        attention_kernel,
        name="attention",
        out_shape=(
            shape((slots, width), bf16),
            shape((slots, width), f32),
            shape((moves, slots, lanes), f32),
            shape((2 * peers, 2 * slots + moves * heads, lanes), bf16),
        ),
        in_specs=[hbm] * 6 + [vmem] * 6,
        out_specs=(vmem,) * 4,
        scratch_shapes=[
            by_slot, by_slot, by_inst, by_move, by_move,
            pltpu.VMEM((2, slots, cached, HEAD), bf16),
            pltpu.VMEM((slots, width + 2 * HEAD), f32),
            pltpu.VMEM((heads, 2 * slots, HEAD), f32),
            pltpu.VMEM((slots, 2 * heads, cached), f32),
            pltpu.VMEM((2 * slots, heads, HEAD), f32),
            pltpu.VMEM((3 * slots, width), f32),
            pltpu.VMEM((slots, lanes), f32),
            pltpu.SemaphoreType.DMA((5 + 2 * slots,)),
        ],
        compiler_params=params,
    )(
        *far(lengths, adapter_ids, move_counts, move_from, move_to, kv_cache),
        *near(ranks, first, second, other, tables, up_other),
    )
    sums = lax.all_to_all(sums, ("inst", "tensor"), 0, 0, axis_index_groups=groups)

    delta1, delta2, attn2 = pl.pallas_call(
        delta_kernel,
        name="deltas",
        out_shape=(shape((slots, width), bf16),) * 3,
        in_specs=[vmem] * 5,
        out_specs=(vmem,) * 3,
        compiler_params=params,
    )(*near(sums, up_own, up_other, attn2_own, landing))
    return (attn1[None], delta1[None], attn2[None], delta2[None])


def solution(mesh):
    row = P("inst", None, "tensor")
    fresh = P("inst", None, None, "tensor")
    whole = P("inst", None, None, None, "tensor")
    return jax.shard_map(
        per_device,
        mesh=mesh,
        in_specs=(row, row, row, row, fresh, fresh, whole, whole, P(), P(), P(), P(), P()),
        out_specs=(row, row, row, row),
        check_vma=False,
    )
```

```python
import math

import jax
import jax.numpy as jnp
from jax import lax
from jax.experimental import pallas as pl
from jax.experimental.pallas import tpu as pltpu
from jax.sharding import PartitionSpec as P

HEAD = 128
masked_score = -1e30
f32 = jnp.float32
bf16 = jnp.bfloat16


def dot_t(a, b):
    return lax.dot_general(a, b, (((1,), (1,)), ((), ())), preferred_element_type=f32)


def dot(a, b):
    return lax.dot_general(a, b, (((1,), (0,)), ((), ())), preferred_element_type=f32)


def twice(table):
    flat = table.reshape(-1, table.shape[-1])
    return jnp.concatenate([flat, flat], 0)


def row_iota(shape):
    return lax.broadcasted_iota(jnp.int32, shape, 0)


def lane_iota(shape):
    return lax.broadcasted_iota(jnp.int32, shape, 1)


def moved_in(base, rows, arrives):
    for r in range(rows.shape[0]):
        taken = arrives[r] > 0.5
        if base.shape[1] != taken.shape[1]:
            taken = jnp.concatenate([taken] * (base.shape[1] // taken.shape[1]), 1)
        base = jnp.where(taken, rows[r : r + 1], base)
    return base


def start_all(pairs, sems, first=0):
    copies = [pltpu.make_async_copy(src, dst, sems.at[first + n]) for n, (src, dst) in enumerate(pairs)]
    for copy in copies:
        copy.start()
    return copies


def wait_all(copies):
    for copy in copies:
        copy.wait()


def halves(value):
    high = value.astype(bf16).astype(f32)
    return jnp.concatenate([high, value - high], 0)


def stage_kernel(
    ids_at, counts_at, leave_at, land_at, lengths_at, h1, h2, q1, q2, f1, f2, tables_at,
    first_out, second_out, tables_out, up_out, arrives_out, adapter_out, lengths_out,
    ids, counts, leave, land, lengths, fresh, fresh_wide, sems,
):
    me = lax.axis_index("inst")
    width = h1.shape[2]
    copies = start_all(
        [
            (f1.at[0], fresh.at[0]), (f2.at[0], fresh.at[1]),
            (h1.at[0], first_out.at[:, :width]), (h2.at[0], second_out.at[:, :width]),
            (q1.at[0], first_out.at[:, width : 2 * width]), (q2.at[0], second_out.at[:, width : 2 * width]),
            (ids_at, ids), (counts_at, counts), (leave_at, leave), (land_at, land), (lengths_at, lengths),
            (tables_at.at[0, :, 3], up_out), (tables_at.at[0], tables_out),
        ],
        sems,
    )
    slots, lanes = adapter_out.shape
    rank = tables_out.shape[2]
    wait_all(copies[:2])
    fresh_wide[...] = fresh[...].astype(f32)
    for step, out in enumerate((first_out, second_out)):
        out[:, 2 * width : 2 * width + HEAD] = fresh_wide[step, :, 0, :].astype(bf16)
        out[:, 2 * width + HEAD :] = fresh_wide[step, :, 1, :].astype(bf16)
    wait_all(copies[6:11])
    row, lane = row_iota((slots, lanes)), lane_iota((slots, lanes))
    adapter = jnp.zeros((slots, lanes), jnp.int32)
    length = jnp.zeros((slots, lanes), jnp.int32)
    target = jnp.full((slots, lanes), -1, jnp.int32)
    for s in range(slots):
        adapter = jnp.where(row == s, ids[s, me], adapter)
        length = jnp.where(row == s, lengths[s, me], length)
    for m in range(leave.shape[0]):
        target = jnp.where((row == leave[m, me]) & (m < counts[me]), land[m, me], target)
    adapter_out[...] = jnp.where(lax.rem(lane, lanes // 2) // rank == adapter, 1.0, 0.0)
    lengths_out[...] = length
    for r in range(slots):
        arrives_out[r] = jnp.where(target == r, 1.0, 0.0)
    wait_all(copies[2:6] + copies[11:])


def rank_kernel(first, second, other, tables, arrives, adapter, out):
    peers, slots, lanes = out.shape
    width = tables.shape[3]
    hidden = [ref[:, :width].astype(f32) for ref in (first, second, other)]
    partials = dot_t(jnp.concatenate(hidden, 0).astype(bf16), twice(tables[:, 0]))
    moved = moved_in(partials[slots : 2 * slots], partials[2 * slots :], arrives)
    both = jnp.where(lane_iota((slots, lanes)) < lanes // 2, partials[:slots], moved)
    both = jnp.where(adapter[...] > 0.5, both, 0.0)
    for peer in range(peers):
        out[peer] = both


def attention_kernel(
    counts_at, leave_at, land_at, kv, ranks, first_rows, second_rows, got_rows, tables, up_other,
    arrives, adapter, lengths,
    attn1_out, own_out, landing_out, sums_out,
    counts, leave, land, queries, scores, mixed, served_rows, rank_rows, sems,
):
    me = lax.axis_index("inst")
    half = lax.axis_size("inst") // 2
    slots, width = attn1_out.shape
    heads = width // HEAD
    cached = kv.shape[3]
    lanes = ranks.shape[2]
    moves = leave.shape[0]
    small = start_all([(counts_at, counts), (leave_at, leave), (land_at, land)], sems)

    lane = lane_iota((slots, lanes))
    low = lane < lanes // 2
    total = ranks[0]
    for peer in range(1, ranks.shape[0]):
        total = total + ranks[peer]
    total = jnp.concatenate([jnp.where(low, total, 0.0), jnp.where(low, 0.0, total)], 0).astype(bf16)
    update = dot(total, twice(tables[:, 1]))
    first = first_rows[:, width:].astype(f32)
    own = second_rows[:, width:].astype(f32)
    second = moved_in(own, got_rows[:, width:].astype(f32), arrives)
    query1 = (first[:, :width] + update[:slots]).astype(bf16).astype(f32)
    query2 = (second[:, :width] + update[slots:]).astype(bf16).astype(f32)
    for h in range(heads):
        columns = slice(h * HEAD, (h + 1) * HEAD)
        queries[h, :slots] = query1[:, columns]
        queries[h, slots:] = query2[:, columns]
    key1, value1 = first[:, width : width + HEAD], first[:, width + HEAD :]
    key2, value2 = second[:, width : width + HEAD], second[:, width + HEAD :]

    scaling = math.log2(math.e) / math.sqrt(HEAD)
    score_shape = (2 * heads, cached)
    position = lane_iota(score_shape)
    extra = (position == cached - 2) | ((position == cached - 1) & (row_iota(score_shape) >= heads))
    last = pl.ds(cached - 16, 16)
    tail_row = row_iota((16, HEAD))

    def with_fresh(tile, one, two):
        tile = jnp.where(tail_row == 14, one, tile.astype(f32))
        return jnp.where(tail_row == 15, two, tile).astype(bf16)

    def with_tail(s, which, one, two):
        body = kv[0, s, which, : cached - 128]
        keep = kv[0, s, which, cached - 128 : cached - 16]
        return body, jnp.concatenate([keep, with_fresh(kv[0, s, which, last, :], one, two)], 0)

    for s in range(slots):
        body, tail = with_tail(s, 0, key1[s : s + 1], key2[s : s + 1])
        query = jnp.concatenate([queries[:, s, :], queries[:, slots + s, :]], 0).astype(bf16)
        score = jnp.concatenate([dot_t(query, body), dot_t(query, tail)], 1) * scaling
        scores[s] = jnp.where((position < lengths[s : s + 1, :1]) | extra, score, masked_score)
    for s in range(slots):
        body, tail = with_tail(s, 1, value1[s : s + 1], value2[s : s + 1])
        score = scores[s]
        weights = jnp.exp2(score - jnp.max(score, 1, keepdims=True))
        probs = (weights * (1.0 / jnp.sum(weights, 1, keepdims=True))).astype(bf16)
        attended = dot(probs[:, : cached - 128], body) + dot(probs[:, cached - 128 :], tail)
        attended = attended.astype(bf16).astype(f32)
        mixed[s] = attended[:heads]
        mixed[slots + s] = attended[heads:]

    vacated = arrives[0]
    for r in range(1, slots):
        vacated = vacated + arrives[r]
    vacated = vacated > 0.5
    for h in range(heads):
        columns = slice(h * HEAD, (h + 1) * HEAD)
        served = mixed[slots:, h, :]
        served_rows[:slots, columns] = mixed[:slots, h, :]
        served_rows[slots : 2 * slots, columns] = jnp.where(vacated, own[:, width + HEAD :], served)
        served_rows[2 * slots :, columns] = served
    stacked = served_rows[...].astype(bf16)
    attn1_out[...] = served_rows[:slots].astype(bf16)
    own_out[...] = served_rows[slots : 2 * slots]

    partials = dot_t(stacked, twice(tables[:, 2]))
    mask = adapter[...] > 0.5
    for_own = jnp.where(mask, jnp.where(low, partials[:slots], partials[slots : 2 * slots]), 0.0)
    rank_rows[...] = jnp.where(mask, partials[2 * slots :], 0.0)
    for_other = jnp.zeros_like(for_own)
    row = row_iota((slots, lanes))
    wait_all(small)
    for m in range(moves):
        lands = (row == land[m, me]) & (m < counts[me])
        for_other = jnp.where(lands, rank_rows[pl.ds(leave[m, me], 1), :], for_other)
    peers = sums_out.shape[0] // 2
    lower = me < half
    for_own, for_other = halves(for_own), halves(for_other)
    in_low = jnp.where(lower, for_own, for_other).astype(bf16)
    in_high = jnp.where(lower, for_other, for_own).astype(bf16)
    sent = jnp.concatenate([mixed[slots + leave[m, me]] for m in range(moves)], 0).astype(bf16)
    for peer in range(peers):
        sums_out[peer, : 2 * slots] = in_low
        sums_out[peers + peer, : 2 * slots] = in_high
        sums_out[peer, 2 * slots :] = sent
        sums_out[peers + peer, 2 * slots :] = sent
    other = jnp.bitwise_xor(me, half)
    for m in range(moves):
        lands = (row == land[m, other]) & (m < counts[other])
        landing_out[m] = jnp.where(lands, 1.0, 0.0)


def delta_kernel(sums, up, up_other, attn1, attn2_own, landing, attn1_out, delta1_out, attn2_out, delta2_out):
    attn1_out[...] = attn1[...]
    lower = lax.axis_index("inst") < lax.axis_size("inst") // 2
    peers = sums.shape[0] // 2
    lanes = sums.shape[2]
    slots, width = attn2_out.shape
    heads = width // HEAD
    moves = landing.shape[0]
    totals = []
    for part in range(2):
        total = sums[part * peers, : 2 * slots].astype(f32)
        for peer in range(1, peers):
            total = total + sums[part * peers + peer, : 2 * slots].astype(f32)
        totals.append(total[:slots] + total[slots:])
    own = jnp.where(lower, totals[0], totals[1])
    got = jnp.where(lower, totals[1], totals[0])
    low = lane_iota((slots, lanes)) < lanes // 2
    rank1 = jnp.where(low, own, 0.0)
    rank2_own = jnp.where(low, pltpu.roll(own, lanes // 2, 1), 0.0)
    rank2_got = jnp.where(low, 0.0, got)
    lands = [landing[m] > 0.5 for m in range(moves)]
    rank2 = rank2_own
    for m in range(moves):
        rank2 = jnp.where(lands[m], rank2_got, rank2)
    table = jnp.concatenate([up[...], up_other[...]], 0)
    delta = dot(jnp.concatenate([rank1, rank2], 0).astype(bf16), table)
    delta1_out[...] = delta[:slots].astype(bf16)
    delta2_out[...] = delta[slots:].astype(bf16)
    sender = jnp.where(lower, peers, 0) + lax.axis_index("tensor")
    moved = sums[sender, 2 * slots :, :].astype(f32)
    for h in range(heads):
        columns = slice(h * HEAD, (h + 1) * HEAD)
        rows = attn2_own[:, columns]
        for m in range(moves):
            rows = jnp.where(lands[m], moved[m * heads + h : m * heads + h + 1], rows)
        attn2_out[:, columns] = rows.astype(bf16)


def per_device(
    query_first,
    query_second,
    hidden_first,
    hidden_second,
    fresh_first,
    fresh_second,
    kv_cache,
    adapters,
    lengths,
    adapter_ids,
    move_counts,
    move_from,
    move_to,
):
    inst_count = lax.axis_size("inst")
    peers = lax.axis_size("tensor")
    half = inst_count // 2
    swap = [(i, i ^ half) for i in range(inst_count)]
    groups = [
        [i * peers + t for t in range(peers)] + [(i + half) * peers + t for t in range(peers)] for i in range(half)
    ]
    _, slots, width = query_first.shape
    _, pool, _, rank, _ = adapters.shape
    moves = move_from.shape[1]
    lanes = 2 * pool * rank
    heads = width // HEAD
    cached = kv_cache.shape[3]
    lengths, adapter_ids, move_from, move_to = lengths.T, adapter_ids.T, move_from.T, move_to.T

    hbm = pl.BlockSpec(memory_space=pltpu.HBM)
    vmem = pl.BlockSpec(memory_space=pltpu.VMEM)
    params = pltpu.CompilerParams(vmem_limit_bytes=16 * 1024 * 1024)

    def shape(dims, dtype):
        return jax.ShapeDtypeStruct(dims, dtype)

    def far(*arrays):
        return [pltpu.with_memory_space_constraint(array, pltpu.HBM) for array in arrays]

    def near(*arrays):
        return [pltpu.with_memory_space_constraint(array, pltpu.VMEM) for array in arrays]

    by_slot = pltpu.SMEM((slots, inst_count), jnp.int32)
    by_inst = pltpu.SMEM((inst_count,), jnp.int32)
    by_move = pltpu.SMEM((moves, inst_count), jnp.int32)
    rows = shape((slots, 2 * width + 2 * HEAD), bf16)

    first, second, tables, up_own, arrives, adapter, slot_lengths = pl.pallas_call(
        stage_kernel,
        name="stage",
        out_shape=(
            rows,
            rows,
            shape(adapters.shape[1:], bf16),
            shape((pool, rank, width), bf16),
            shape((slots, slots, lanes), f32),
            shape((slots, lanes), f32),
            shape((slots, lanes), jnp.int32),
        ),
        in_specs=[hbm] * 12,
        out_specs=(vmem,) * 7,
        scratch_shapes=[
            by_slot, by_inst, by_move, by_move, by_slot,
            pltpu.VMEM((2, slots, 2, HEAD), bf16),
            pltpu.VMEM((2, slots, 2, HEAD), f32),
            pltpu.SemaphoreType.DMA((13,)),
        ],
        compiler_params=params,
    )(
        *far(
            adapter_ids, move_counts, move_from, move_to, lengths,
            hidden_first, hidden_second, query_first, query_second, fresh_first, fresh_second, adapters,
        )
    )
    up_own = up_own.reshape(pool * rank, width)
    up_other = lax.ppermute(up_own, "inst", swap)
    other = lax.ppermute(second, "inst", swap)

    ranks = pl.pallas_call(
        rank_kernel,
        name="rank_partials",
        out_shape=shape((peers, slots, lanes), f32),
        in_specs=[vmem] * 6,
        out_specs=vmem,
        cost_estimate=pl.CostEstimate(flops=2 * 10**10, bytes_accessed=10**8, transcendentals=0),
        compiler_params=params,
    )(*near(first, second, other, tables, arrives, adapter))
    ranks = lax.all_to_all(ranks, "tensor", 0, 0)

    attn1, attn2_own, landing, sums = pl.pallas_call(
        attention_kernel,
        name="attention",
        out_shape=(
            shape((slots, width), bf16),
            shape((slots, width), f32),
            shape((moves, slots, lanes), f32),
            shape((2 * peers, 2 * slots + moves * heads, lanes), bf16),
        ),
        in_specs=[hbm] * 3 + [vmem] * 10,
        out_specs=(vmem,) * 4,
        scratch_shapes=[
            by_inst, by_move, by_move,
            pltpu.VMEM((heads, 2 * slots, HEAD), f32),
            pltpu.VMEM((slots, 2 * heads, cached), f32),
            pltpu.VMEM((2 * slots, heads, HEAD), f32),
            pltpu.VMEM((3 * slots, width), f32),
            pltpu.VMEM((slots, lanes), f32),
            pltpu.SemaphoreType.DMA((3,)),
        ],
        compiler_params=params,
    )(
        *far(move_counts, move_from, move_to),
        *near(kv_cache, ranks, first, second, other, tables, up_other, arrives, adapter, slot_lengths),
    )
    sums = lax.all_to_all(sums, ("inst", "tensor"), 0, 0, axis_index_groups=groups)

    attn1, delta1, attn2, delta2 = pl.pallas_call(
        delta_kernel,
        name="deltas",
        out_shape=(shape((slots, width), bf16),) * 4,
        in_specs=[vmem] * 6,
        out_specs=(vmem,) * 4,
        compiler_params=params,
    )(*near(sums, up_own, up_other, attn1, attn2_own, landing))
    return (attn1[None], delta1[None], attn2[None], delta2[None])


def solution(mesh):
    row = P("inst", None, "tensor")
    fresh = P("inst", None, None, "tensor")
    whole = P("inst", None, None, None, "tensor")
    return jax.shard_map(
        per_device,
        mesh=mesh,
        in_specs=(row, row, row, row, fresh, fresh, whole, whole, P(), P(), P(), P(), P()),
        out_specs=(row, row, row, row),
        check_vma=False,
    )
```

```python
import math

import jax
import jax.numpy as jnp
from jax import lax
from jax.experimental import pallas as pl
from jax.experimental.pallas import tpu as pltpu
from jax.sharding import PartitionSpec as P

HEAD = 128
masked_score = -1e30
f32 = jnp.float32
bf16 = jnp.bfloat16


def dot_t(a, b):
    return lax.dot_general(a, b, (((1,), (1,)), ((), ())), preferred_element_type=f32)


def dot(a, b):
    return lax.dot_general(a, b, (((1,), (0,)), ((), ())), preferred_element_type=f32)


def twice(table):
    flat = table.reshape(-1, table.shape[-1])
    return jnp.concatenate([flat, flat], 0)


def row_iota(shape):
    return lax.broadcasted_iota(jnp.int32, shape, 0)


def lane_iota(shape):
    return lax.broadcasted_iota(jnp.int32, shape, 1)


def moved_in(base, rows, arrives):
    for r in range(rows.shape[0]):
        taken = arrives[r] > 0.5
        if base.shape[1] != taken.shape[1]:
            taken = jnp.concatenate([taken] * (base.shape[1] // taken.shape[1]), 1)
        base = jnp.where(taken, rows[r : r + 1], base)
    return base


def start_all(pairs, sems, first=0):
    copies = [pltpu.make_async_copy(src, dst, sems.at[first + n]) for n, (src, dst) in enumerate(pairs)]
    for copy in copies:
        copy.start()
    return copies


def wait_all(copies):
    for copy in copies:
        copy.wait()


def halves(value):
    high = value.astype(bf16).astype(f32)
    return jnp.concatenate([high, value - high], 0)


def stage_kernel(
    ids_at, counts_at, leave_at, land_at, lengths_at, h1, h2, q1, q2, f1, f2, tables_at,
    first_out, second_out, tables_out, up_out, arrives_out, adapter_out, lengths_out,
    ids, counts, leave, land, lengths, fresh, fresh_wide, sems,
):
    me = lax.axis_index("inst")
    width = h1.shape[2]
    copies = start_all(
        [
            (f1.at[0], fresh.at[0]), (f2.at[0], fresh.at[1]),
            (h1.at[0], first_out.at[:, :width]), (h2.at[0], second_out.at[:, :width]),
            (q1.at[0], first_out.at[:, width : 2 * width]), (q2.at[0], second_out.at[:, width : 2 * width]),
            (ids_at, ids), (counts_at, counts), (leave_at, leave), (land_at, land), (lengths_at, lengths),
            (tables_at.at[0, :, 3], up_out), (tables_at.at[0], tables_out),
        ],
        sems,
    )
    slots, lanes = adapter_out.shape
    rank = tables_out.shape[2]
    wait_all(copies[:2])
    fresh_wide[...] = fresh[...].astype(f32)
    for step, out in enumerate((first_out, second_out)):
        out[:, 2 * width : 2 * width + HEAD] = fresh_wide[step, :, 0, :].astype(bf16)
        out[:, 2 * width + HEAD :] = fresh_wide[step, :, 1, :].astype(bf16)
    wait_all(copies[6:11])
    row, lane = row_iota((slots, lanes)), lane_iota((slots, lanes))
    adapter = jnp.zeros((slots, lanes), jnp.int32)
    length = jnp.zeros((slots, lanes), jnp.int32)
    target = jnp.full((slots, lanes), -1, jnp.int32)
    for s in range(slots):
        adapter = jnp.where(row == s, ids[s, me], adapter)
        length = jnp.where(row == s, lengths[s, me], length)
    for m in range(leave.shape[0]):
        target = jnp.where((row == leave[m, me]) & (m < counts[me]), land[m, me], target)
    adapter_out[...] = jnp.where(lax.rem(lane, lanes // 2) // rank == adapter, 1.0, 0.0)
    lengths_out[...] = length
    for r in range(slots):
        arrives_out[r] = jnp.where(target == r, 1.0, 0.0)
    wait_all(copies[2:6] + copies[11:])


def rank_kernel(first, second, other, tables, arrives, adapter, out):
    peers, slots, lanes = out.shape
    width = tables.shape[3]
    hidden = [ref[:, :width].astype(f32) for ref in (first, second, other)]
    partials = dot_t(jnp.concatenate(hidden, 0).astype(bf16), twice(tables[:, 0]))
    moved = moved_in(partials[slots : 2 * slots], partials[2 * slots :], arrives)
    both = jnp.where(lane_iota((slots, lanes)) < lanes // 2, partials[:slots], moved)
    both = jnp.where(adapter[...] > 0.5, both, 0.0)
    for peer in range(peers):
        out[peer] = both


def attention_kernel(
    counts_at, leave_at, land_at, kv, ranks, first_rows, second_rows, got_rows, tables, up_other,
    arrives, adapter, lengths,
    attn1_out, own_out, landing_out, sums_out,
    counts, leave, land, queries, scores, mixed, served_rows, rank_rows, sems,
):
    me = lax.axis_index("inst")
    half = lax.axis_size("inst") // 2
    slots, width = attn1_out.shape
    heads = width // HEAD
    cached = kv.shape[3]
    lanes = ranks.shape[2]
    moves = leave.shape[0]
    small = start_all([(counts_at, counts), (leave_at, leave), (land_at, land)], sems)

    lane = lane_iota((slots, lanes))
    low = lane < lanes // 2
    total = ranks[0]
    for peer in range(1, ranks.shape[0]):
        total = total + ranks[peer]
    total = jnp.concatenate([jnp.where(low, total, 0.0), jnp.where(low, 0.0, total)], 0).astype(bf16)
    update = dot(total, twice(tables[:, 1]))
    first = first_rows[:, width:].astype(f32)
    own = second_rows[:, width:].astype(f32)
    second = moved_in(own, got_rows[:, width:].astype(f32), arrives)
    query1 = (first[:, :width] + update[:slots]).astype(bf16).astype(f32)
    query2 = (second[:, :width] + update[slots:]).astype(bf16).astype(f32)
    for h in range(heads):
        columns = slice(h * HEAD, (h + 1) * HEAD)
        queries[h, :slots] = query1[:, columns]
        queries[h, slots:] = query2[:, columns]
    key1, value1 = first[:, width : width + HEAD], first[:, width + HEAD :]
    key2, value2 = second[:, width : width + HEAD], second[:, width + HEAD :]

    scaling = math.log2(math.e) / math.sqrt(HEAD)
    score_shape = (2 * heads, cached)
    position = lane_iota(score_shape)
    extra = (position == cached - 2) | ((position == cached - 1) & (row_iota(score_shape) >= heads))
    last = pl.ds(cached - 16, 16)
    tail_row = row_iota((16, HEAD))

    def with_fresh(tile, one, two):
        tile = jnp.where(tail_row == 14, one, tile.astype(f32))
        return jnp.where(tail_row == 15, two, tile).astype(bf16)

    def with_tail(s, which, one, two):
        body = kv[0, s, which, : cached - 128]
        keep = kv[0, s, which, cached - 128 : cached - 16]
        return body, jnp.concatenate([keep, with_fresh(kv[0, s, which, last, :], one, two)], 0)

    for s in range(slots):
        body, tail = with_tail(s, 0, key1[s : s + 1], key2[s : s + 1])
        query = jnp.concatenate([queries[:, s, :], queries[:, slots + s, :]], 0).astype(bf16)
        score = jnp.concatenate([dot_t(query, body), dot_t(query, tail)], 1) * scaling
        scores[s] = jnp.where((position < lengths[s : s + 1, :1]) | extra, score, masked_score)
    for s in range(slots):
        body, tail = with_tail(s, 1, value1[s : s + 1], value2[s : s + 1])
        score = scores[s]
        weights = jnp.exp2(score - jnp.max(score, 1, keepdims=True))
        probs = (weights * (1.0 / jnp.sum(weights, 1, keepdims=True))).astype(bf16)
        attended = dot(probs[:, : cached - 128], body) + dot(probs[:, cached - 128 :], tail)
        attended = attended.astype(bf16).astype(f32)
        mixed[s] = attended[:heads]
        mixed[slots + s] = attended[heads:]

    vacated = arrives[0]
    for r in range(1, slots):
        vacated = vacated + arrives[r]
    vacated = vacated > 0.5
    for h in range(heads):
        columns = slice(h * HEAD, (h + 1) * HEAD)
        served = mixed[slots:, h, :]
        served_rows[:slots, columns] = mixed[:slots, h, :]
        served_rows[slots : 2 * slots, columns] = jnp.where(vacated, own[:, width + HEAD :], served)
        served_rows[2 * slots :, columns] = served
    stacked = served_rows[...].astype(bf16)
    attn1_out[...] = served_rows[:slots].astype(bf16)
    own_out[...] = served_rows[slots : 2 * slots]

    partials = dot_t(stacked, twice(tables[:, 2]))
    mask = adapter[...] > 0.5
    for_own = jnp.where(mask, jnp.where(low, partials[:slots], partials[slots : 2 * slots]), 0.0)
    rank_rows[...] = jnp.where(mask, partials[2 * slots :], 0.0)
    for_other = jnp.zeros_like(for_own)
    row = row_iota((slots, lanes))
    wait_all(small)
    for m in range(moves):
        lands = (row == land[m, me]) & (m < counts[me])
        for_other = jnp.where(lands, rank_rows[pl.ds(leave[m, me], 1), :], for_other)
    peers = sums_out.shape[0] // 2
    lower = me < half
    for_own, for_other = halves(for_own), halves(for_other)
    in_low = jnp.where(lower, for_own, for_other).astype(bf16)
    in_high = jnp.where(lower, for_other, for_own).astype(bf16)
    sent = jnp.concatenate([mixed[slots + leave[m, me]] for m in range(moves)], 0).astype(bf16)
    for peer in range(peers):
        sums_out[peer, : 2 * slots] = in_low
        sums_out[peers + peer, : 2 * slots] = in_high
        sums_out[peer, 2 * slots :] = sent
        sums_out[peers + peer, 2 * slots :] = sent
    other = jnp.bitwise_xor(me, half)
    for m in range(moves):
        lands = (row == land[m, other]) & (m < counts[other])
        landing_out[m] = jnp.where(lands, 1.0, 0.0)


def delta_kernel(sums, up, up_other, attn1, attn2_own, landing, attn1_out, delta1_out, attn2_out, delta2_out):
    attn1_out[...] = attn1[...]
    lower = lax.axis_index("inst") < lax.axis_size("inst") // 2
    peers = sums.shape[0] // 2
    lanes = sums.shape[2]
    slots, width = attn2_out.shape
    heads = width // HEAD
    moves = landing.shape[0]
    totals = []
    for part in range(2):
        total = sums[part * peers, : 2 * slots].astype(f32)
        for peer in range(1, peers):
            total = total + sums[part * peers + peer, : 2 * slots].astype(f32)
        totals.append(total[:slots] + total[slots:])
    own = jnp.where(lower, totals[0], totals[1])
    got = jnp.where(lower, totals[1], totals[0])
    low = lane_iota((slots, lanes)) < lanes // 2
    rank1 = jnp.where(low, own, 0.0)
    rank2_own = jnp.where(low, pltpu.roll(own, lanes // 2, 1), 0.0)
    rank2_got = jnp.where(low, 0.0, got)
    lands = [landing[m] > 0.5 for m in range(moves)]
    rank2 = rank2_own
    for m in range(moves):
        rank2 = jnp.where(lands[m], rank2_got, rank2)
    table = jnp.concatenate([up[...], up_other[...]], 0)
    delta = dot(jnp.concatenate([rank1, rank2], 0).astype(bf16), table)
    delta1_out[...] = delta[:slots].astype(bf16)
    delta2_out[...] = delta[slots:].astype(bf16)
    sender = jnp.where(lower, peers, 0) + peers - 1 - lax.axis_index("tensor")
    moved = sums[sender, 2 * slots :, :].astype(f32)
    for h in range(heads):
        columns = slice(h * HEAD, (h + 1) * HEAD)
        rows = attn2_own[:, columns]
        for m in range(moves):
            rows = jnp.where(lands[m], moved[m * heads + h : m * heads + h + 1], rows)
        attn2_out[:, columns] = rows.astype(bf16)


def per_device(
    query_first,
    query_second,
    hidden_first,
    hidden_second,
    fresh_first,
    fresh_second,
    kv_cache,
    adapters,
    lengths,
    adapter_ids,
    move_counts,
    move_from,
    move_to,
):
    inst_count = lax.axis_size("inst")
    peers = lax.axis_size("tensor")
    half = inst_count // 2
    swap = [(i, i ^ half) for i in range(inst_count)]
    teams = [[i * peers + t for t in reversed(range(peers))] for i in range(inst_count)]
    pairs = [teams[i] + teams[i + half] for i in range(half)]
    _, slots, width = query_first.shape
    _, pool, _, rank, _ = adapters.shape
    moves = move_from.shape[1]
    lanes = 2 * pool * rank
    heads = width // HEAD
    cached = kv_cache.shape[3]
    lengths, adapter_ids, move_from, move_to = lengths.T, adapter_ids.T, move_from.T, move_to.T

    hbm = pl.BlockSpec(memory_space=pltpu.HBM)
    vmem = pl.BlockSpec(memory_space=pltpu.VMEM)
    params = pltpu.CompilerParams(vmem_limit_bytes=16 * 1024 * 1024)

    def shape(dims, dtype):
        return jax.ShapeDtypeStruct(dims, dtype)

    def far(*arrays):
        return [pltpu.with_memory_space_constraint(array, pltpu.HBM) for array in arrays]

    def near(*arrays):
        return [pltpu.with_memory_space_constraint(array, pltpu.VMEM) for array in arrays]

    by_slot = pltpu.SMEM((slots, inst_count), jnp.int32)
    by_inst = pltpu.SMEM((inst_count,), jnp.int32)
    by_move = pltpu.SMEM((moves, inst_count), jnp.int32)
    rows = shape((slots, 2 * width + 2 * HEAD), bf16)

    first, second, tables, up_own, arrives, adapter, slot_lengths = pl.pallas_call(
        stage_kernel,
        name="stage",
        out_shape=(
            rows,
            rows,
            shape(adapters.shape[1:], bf16),
            shape((pool, rank, width), bf16),
            shape((slots, slots, lanes), f32),
            shape((slots, lanes), f32),
            shape((slots, lanes), jnp.int32),
        ),
        in_specs=[hbm] * 12,
        out_specs=(vmem,) * 7,
        scratch_shapes=[
            by_slot, by_inst, by_move, by_move, by_slot,
            pltpu.VMEM((2, slots, 2, HEAD), bf16),
            pltpu.VMEM((2, slots, 2, HEAD), f32),
            pltpu.SemaphoreType.DMA((13,)),
        ],
        compiler_params=params,
    )(
        *far(
            adapter_ids, move_counts, move_from, move_to, lengths,
            hidden_first, hidden_second, query_first, query_second, fresh_first, fresh_second, adapters,
        )
    )
    up_own = up_own.reshape(pool * rank, width)
    up_other = lax.ppermute(up_own, "inst", swap)
    other = lax.ppermute(second, "inst", swap)

    ranks = pl.pallas_call(
        rank_kernel,
        name="rank_partials",
        out_shape=shape((peers, slots, lanes), f32),
        in_specs=[vmem] * 6,
        out_specs=vmem,
        cost_estimate=pl.CostEstimate(flops=2 * 10**10, bytes_accessed=10**8, transcendentals=0),
        compiler_params=params,
    )(*near(first, second, other, tables, arrives, adapter))
    ranks = lax.all_to_all(ranks, ("inst", "tensor"), 0, 0, axis_index_groups=teams)

    attn1, attn2_own, landing, sums = pl.pallas_call(
        attention_kernel,
        name="attention",
        out_shape=(
            shape((slots, width), bf16),
            shape((slots, width), f32),
            shape((moves, slots, lanes), f32),
            shape((2 * peers, 2 * slots + moves * heads, lanes), bf16),
        ),
        in_specs=[hbm] * 3 + [vmem] * 10,
        out_specs=(vmem,) * 4,
        scratch_shapes=[
            by_inst, by_move, by_move,
            pltpu.VMEM((heads, 2 * slots, HEAD), f32),
            pltpu.VMEM((slots, 2 * heads, cached), f32),
            pltpu.VMEM((2 * slots, heads, HEAD), f32),
            pltpu.VMEM((3 * slots, width), f32),
            pltpu.VMEM((slots, lanes), f32),
            pltpu.SemaphoreType.DMA((3,)),
        ],
        compiler_params=params,
    )(
        *far(move_counts, move_from, move_to),
        *near(kv_cache, ranks, first, second, other, tables, up_other, arrives, adapter, slot_lengths),
    )
    sums = lax.all_to_all(sums, ("inst", "tensor"), 0, 0, axis_index_groups=pairs)

    attn1, delta1, attn2, delta2 = pl.pallas_call(
        delta_kernel,
        name="deltas",
        out_shape=(shape((slots, width), bf16),) * 4,
        in_specs=[vmem] * 6,
        out_specs=(vmem,) * 4,
        compiler_params=params,
    )(*near(sums, up_own, up_other, attn1, attn2_own, landing))
    return (attn1[None], delta1[None], attn2[None], delta2[None])


def solution(mesh):
    row = P("inst", None, "tensor")
    fresh = P("inst", None, None, "tensor")
    whole = P("inst", None, None, None, "tensor")
    return jax.shard_map(
        per_device,
        mesh=mesh,
        in_specs=(row, row, row, row, fresh, fresh, whole, whole, P(), P(), P(), P(), P()),
        out_specs=(row, row, row, row),
        check_vma=False,
    )
```

```python
import math

import jax
import jax.numpy as jnp
from jax import lax
from jax.experimental import pallas as pl
from jax.experimental.pallas import tpu as pltpu
from jax.sharding import PartitionSpec as P

HEAD = 128
masked_score = -1e30
f32 = jnp.float32
bf16 = jnp.bfloat16


def dot_t(a, b):
    return lax.dot_general(a, b, (((1,), (1,)), ((), ())), preferred_element_type=f32)


def dot(a, b):
    return lax.dot_general(a, b, (((1,), (0,)), ((), ())), preferred_element_type=f32)


def twice(table):
    flat = table.reshape(-1, table.shape[-1])
    return jnp.concatenate([flat, flat], 0)


def row_iota(shape):
    return lax.broadcasted_iota(jnp.int32, shape, 0)


def lane_iota(shape):
    return lax.broadcasted_iota(jnp.int32, shape, 1)


def moved_in(base, rows, arrives):
    for r in range(rows.shape[0]):
        taken = arrives[r] > 0.5
        if base.shape[1] != taken.shape[1]:
            taken = jnp.concatenate([taken] * (base.shape[1] // taken.shape[1]), 1)
        base = jnp.where(taken, rows[r : r + 1], base)
    return base


def start_all(pairs, sems, first=0):
    copies = [pltpu.make_async_copy(src, dst, sems.at[first + n]) for n, (src, dst) in enumerate(pairs)]
    for copy in copies:
        copy.start()
    return copies


def wait_all(copies):
    for copy in copies:
        copy.wait()


def halves(value):
    high = value.astype(bf16).astype(f32)
    return jnp.concatenate([high, value - high], 0)


def stage_kernel(
    ids_at, counts_at, leave_at, land_at, lengths_at, h1, h2, q1, q2, f1, f2, tables_at,
    first_out, second_out, tables_out, parcel_out, arrives_out, adapter_out, lengths_out,
    ids, counts, leave, land, lengths, fresh, fresh_wide, sems,
):
    me = lax.axis_index("inst")
    width = h1.shape[2]
    copies = start_all(
        [
            (f1.at[0], fresh.at[0]), (f2.at[0], fresh.at[1]),
            (h1.at[0], first_out.at[:, :width]), (h2.at[0], second_out.at[:, :width]),
            (q1.at[0], first_out.at[:, width : 2 * width]), (q2.at[0], second_out.at[:, width : 2 * width]),
            (ids_at, ids), (counts_at, counts), (leave_at, leave), (land_at, land), (lengths_at, lengths),
            (tables_at.at[0], tables_out),
        ],
        sems,
    )
    slots, lanes = adapter_out.shape
    rank = tables_out.shape[2]
    wait_all(copies[:2])
    fresh_wide[...] = fresh[...].astype(f32)
    for step, out in enumerate((first_out, second_out)):
        out[:, 2 * width : 2 * width + HEAD] = fresh_wide[step, :, 0, :].astype(bf16)
        out[:, 2 * width + HEAD :] = fresh_wide[step, :, 1, :].astype(bf16)
    wait_all(copies[6:11])
    row, lane = row_iota((slots, lanes)), lane_iota((slots, lanes))
    adapter = jnp.zeros((slots, lanes), jnp.int32)
    length = jnp.zeros((slots, lanes), jnp.int32)
    target = jnp.full((slots, lanes), -1, jnp.int32)
    for s in range(slots):
        adapter = jnp.where(row == s, ids[s, me], adapter)
        length = jnp.where(row == s, lengths[s, me], length)
    for m in range(leave.shape[0]):
        target = jnp.where((row == leave[m, me]) & (m < counts[me]), land[m, me], target)
    adapter_out[...] = jnp.where(lax.rem(lane, lanes // 2) // rank == adapter, 1.0, 0.0)
    lengths_out[...] = length
    for r in range(slots):
        arrives_out[r] = jnp.where(target == r, 1.0, 0.0)
    wait_all(copies[2:6] + copies[11:])
    ups = tables_out[:, 3].reshape(-1, width)
    parcel_out[: ups.shape[0]] = ups
    fresh_rows = second_out[:, 2 * width :].astype(f32)
    fresh_rows = jnp.concatenate([fresh_rows, jnp.zeros((slots, width - 2 * HEAD), f32)], 1)
    tail = jnp.concatenate([second_out[:, width : 2 * width].astype(f32), fresh_rows], 0)
    parcel_out[ups.shape[0] :] = tail.astype(bf16)


def rank_kernel(first, second, hidden_other, tables, arrives, adapter, out):
    peers, slots, lanes = out.shape
    width = tables.shape[3]
    hidden = [ref[:, :width].astype(f32) for ref in (first, second, hidden_other)]
    partials = dot_t(jnp.concatenate(hidden, 0).astype(bf16), twice(tables[:, 0]))
    moved = moved_in(partials[slots : 2 * slots], partials[2 * slots :], arrives)
    both = jnp.where(lane_iota((slots, lanes)) < lanes // 2, partials[:slots], moved)
    both = jnp.where(adapter[...] > 0.5, both, 0.0)
    for peer in range(peers):
        out[peer] = both


def attention_kernel(
    counts_at, leave_at, land_at, kv, ranks, first_rows, second_rows, parcel, tables,
    arrives, adapter, lengths,
    attn1_out, own_out, landing_out, sums_out,
    counts, leave, land, queries, scores, mixed, served_rows, rank_rows, sems,
):
    me = lax.axis_index("inst")
    half = lax.axis_size("inst") // 2
    slots, width = attn1_out.shape
    heads = width // HEAD
    cached = kv.shape[3]
    lanes = ranks.shape[2]
    moves = leave.shape[0]
    small = start_all([(counts_at, counts), (leave_at, leave), (land_at, land)], sems)

    lane = lane_iota((slots, lanes))
    low = lane < lanes // 2
    total = ranks[0]
    for peer in range(1, ranks.shape[0]):
        total = total + ranks[peer]
    total = jnp.concatenate([jnp.where(low, total, 0.0), jnp.where(low, 0.0, total)], 0).astype(bf16)
    update = dot(total, twice(tables[:, 1]))
    first = first_rows[:, width:].astype(f32)
    own = second_rows[:, width:].astype(f32)
    got = parcel[pl.ds(parcel.shape[0] - 2 * slots, 2 * slots), :].astype(f32)
    second = moved_in(own, jnp.concatenate([got[:slots], got[slots:, : 2 * HEAD]], 1), arrives)
    query1 = (first[:, :width] + update[:slots]).astype(bf16).astype(f32)
    query2 = (second[:, :width] + update[slots:]).astype(bf16).astype(f32)
    for h in range(heads):
        columns = slice(h * HEAD, (h + 1) * HEAD)
        queries[h, :slots] = query1[:, columns]
        queries[h, slots:] = query2[:, columns]
    key1, value1 = first[:, width : width + HEAD], first[:, width + HEAD :]
    key2, value2 = second[:, width : width + HEAD], second[:, width + HEAD :]

    scaling = math.log2(math.e) / math.sqrt(HEAD)
    score_shape = (2 * heads, cached)
    position = lane_iota(score_shape)
    extra = (position == cached - 2) | ((position == cached - 1) & (row_iota(score_shape) >= heads))
    last = pl.ds(cached - 16, 16)
    tail_row = row_iota((16, HEAD))

    def with_fresh(tile, one, two):
        tile = jnp.where(tail_row == 14, one, tile.astype(f32))
        return jnp.where(tail_row == 15, two, tile).astype(bf16)

    def with_tail(s, which, one, two):
        body = kv[0, s, which, : cached - 128]
        keep = kv[0, s, which, cached - 128 : cached - 16]
        return body, jnp.concatenate([keep, with_fresh(kv[0, s, which, last, :], one, two)], 0)

    for s in range(slots):
        body, tail = with_tail(s, 0, key1[s : s + 1], key2[s : s + 1])
        query = jnp.concatenate([queries[:, s, :], queries[:, slots + s, :]], 0).astype(bf16)
        score = jnp.concatenate([dot_t(query, body), dot_t(query, tail)], 1) * scaling
        scores[s] = jnp.where((position < lengths[s : s + 1, :1]) | extra, score, masked_score)
    for s in range(slots):
        body, tail = with_tail(s, 1, value1[s : s + 1], value2[s : s + 1])
        score = scores[s]
        weights = jnp.exp2(score - jnp.max(score, 1, keepdims=True))
        probs = (weights * (1.0 / jnp.sum(weights, 1, keepdims=True))).astype(bf16)
        attended = dot(probs[:, : cached - 128], body) + dot(probs[:, cached - 128 :], tail)
        attended = attended.astype(bf16).astype(f32)
        mixed[s] = attended[:heads]
        mixed[slots + s] = attended[heads:]

    vacated = arrives[0]
    for r in range(1, slots):
        vacated = vacated + arrives[r]
    vacated = vacated > 0.5
    for h in range(heads):
        columns = slice(h * HEAD, (h + 1) * HEAD)
        served = mixed[slots:, h, :]
        served_rows[:slots, columns] = mixed[:slots, h, :]
        served_rows[slots : 2 * slots, columns] = jnp.where(vacated, own[:, width + HEAD :], served)
        served_rows[2 * slots :, columns] = served
    stacked = served_rows[...].astype(bf16)
    attn1_out[...] = served_rows[:slots].astype(bf16)
    own_out[...] = served_rows[slots : 2 * slots]

    partials = dot_t(stacked, twice(tables[:, 2]))
    mask = adapter[...] > 0.5
    for_own = jnp.where(mask, jnp.where(low, partials[:slots], partials[slots : 2 * slots]), 0.0)
    rank_rows[...] = jnp.where(mask, partials[2 * slots :], 0.0)
    for_other = jnp.zeros_like(for_own)
    row = row_iota((slots, lanes))
    wait_all(small)
    for m in range(moves):
        lands = (row == land[m, me]) & (m < counts[me])
        for_other = jnp.where(lands, rank_rows[pl.ds(leave[m, me], 1), :], for_other)
    peers = sums_out.shape[0] // 2
    lower = me < half
    for_own, for_other = halves(for_own), halves(for_other)
    in_low = jnp.where(lower, for_own, for_other).astype(bf16)
    in_high = jnp.where(lower, for_other, for_own).astype(bf16)
    sent = jnp.concatenate([mixed[slots + leave[m, me]] for m in range(moves)], 0).astype(bf16)
    for peer in range(peers):
        sums_out[peer, : 2 * slots] = in_low
        sums_out[peers + peer, : 2 * slots] = in_high
        sums_out[peer, 2 * slots :] = sent
        sums_out[peers + peer, 2 * slots :] = sent
    other = jnp.bitwise_xor(me, half)
    for m in range(moves):
        lands = (row == land[m, other]) & (m < counts[other])
        landing_out[m] = jnp.where(lands, 1.0, 0.0)


def delta_kernel(sums, tables, parcel, attn1, attn2_own, landing, attn1_out, delta1_out, attn2_out, delta2_out):
    attn1_out[...] = attn1[...]
    lower = lax.axis_index("inst") < lax.axis_size("inst") // 2
    peers = sums.shape[0] // 2
    lanes = sums.shape[2]
    slots, width = attn2_out.shape
    heads = width // HEAD
    moves = landing.shape[0]
    totals = []
    for part in range(2):
        total = sums[part * peers, : 2 * slots].astype(f32)
        for peer in range(1, peers):
            total = total + sums[part * peers + peer, : 2 * slots].astype(f32)
        totals.append(total[:slots] + total[slots:])
    own = jnp.where(lower, totals[0], totals[1])
    got = jnp.where(lower, totals[1], totals[0])
    low = lane_iota((slots, lanes)) < lanes // 2
    rank1 = jnp.where(low, own, 0.0)
    rank2_own = jnp.where(low, pltpu.roll(own, lanes // 2, 1), 0.0)
    rank2_got = jnp.where(low, 0.0, got)
    lands = [landing[m] > 0.5 for m in range(moves)]
    rank2 = rank2_own
    for m in range(moves):
        rank2 = jnp.where(lands[m], rank2_got, rank2)
    ups = tables[:, 3].reshape(-1, width)
    table = jnp.concatenate([ups, parcel[: ups.shape[0]]], 0)
    delta = dot(jnp.concatenate([rank1, rank2], 0).astype(bf16), table)
    delta1_out[...] = delta[:slots].astype(bf16)
    delta2_out[...] = delta[slots:].astype(bf16)
    sender = jnp.where(lower, peers, 0) + peers - 1 - lax.axis_index("tensor")
    moved = sums[sender, 2 * slots :, :].astype(f32)
    for h in range(heads):
        columns = slice(h * HEAD, (h + 1) * HEAD)
        rows = attn2_own[:, columns]
        for m in range(moves):
            rows = jnp.where(lands[m], moved[m * heads + h : m * heads + h + 1], rows)
        attn2_out[:, columns] = rows.astype(bf16)


def per_device(
    query_first,
    query_second,
    hidden_first,
    hidden_second,
    fresh_first,
    fresh_second,
    kv_cache,
    adapters,
    lengths,
    adapter_ids,
    move_counts,
    move_from,
    move_to,
):
    inst_count = lax.axis_size("inst")
    peers = lax.axis_size("tensor")
    half = inst_count // 2
    swap = [(i, i ^ half) for i in range(inst_count)]
    teams = [[i * peers + t for t in reversed(range(peers))] for i in range(inst_count)]
    pairs = [teams[i] + teams[i + half] for i in range(half)]
    _, slots, width = query_first.shape
    _, pool, _, rank, _ = adapters.shape
    moves = move_from.shape[1]
    lanes = 2 * pool * rank
    heads = width // HEAD
    cached = kv_cache.shape[3]
    lengths, adapter_ids, move_from, move_to = lengths.T, adapter_ids.T, move_from.T, move_to.T

    hbm = pl.BlockSpec(memory_space=pltpu.HBM)
    vmem = pl.BlockSpec(memory_space=pltpu.VMEM)
    params = pltpu.CompilerParams(vmem_limit_bytes=16 * 1024 * 1024)

    def shape(dims, dtype):
        return jax.ShapeDtypeStruct(dims, dtype)

    def far(*arrays):
        return [pltpu.with_memory_space_constraint(array, pltpu.HBM) for array in arrays]

    def near(*arrays):
        return [pltpu.with_memory_space_constraint(array, pltpu.VMEM) for array in arrays]

    by_slot = pltpu.SMEM((slots, inst_count), jnp.int32)
    by_inst = pltpu.SMEM((inst_count,), jnp.int32)
    by_move = pltpu.SMEM((moves, inst_count), jnp.int32)
    rows = shape((slots, 2 * width + 2 * HEAD), bf16)

    first, second, tables, parcel, arrives, adapter, slot_lengths = pl.pallas_call(
        stage_kernel,
        name="stage",
        out_shape=(
            rows,
            rows,
            shape(adapters.shape[1:], bf16),
            shape((pool * rank + 2 * slots, width), bf16),
            shape((slots, slots, lanes), f32),
            shape((slots, lanes), f32),
            shape((slots, lanes), jnp.int32),
        ),
        in_specs=[hbm] * 12,
        out_specs=(vmem,) * 7,
        scratch_shapes=[
            by_slot, by_inst, by_move, by_move, by_slot,
            pltpu.VMEM((2, slots, 2, HEAD), bf16),
            pltpu.VMEM((2, slots, 2, HEAD), f32),
            pltpu.SemaphoreType.DMA((12,)),
        ],
        compiler_params=params,
    )(
        *far(
            adapter_ids, move_counts, move_from, move_to, lengths,
            hidden_first, hidden_second, query_first, query_second, fresh_first, fresh_second, adapters,
        )
    )
    parcel_other = lax.ppermute(parcel, "inst", swap)
    hidden_other = lax.ppermute(hidden_second[0], "inst", swap)

    ranks = pl.pallas_call(
        rank_kernel,
        name="rank_partials",
        out_shape=shape((peers, slots, lanes), f32),
        in_specs=[vmem] * 6,
        out_specs=vmem,
        cost_estimate=pl.CostEstimate(flops=2 * 10**10, bytes_accessed=10**8, transcendentals=0),
        compiler_params=params,
    )(*near(first, second, hidden_other, tables, arrives, adapter))
    ranks = lax.all_to_all(ranks, ("inst", "tensor"), 0, 0, axis_index_groups=teams)

    attn1, attn2_own, landing, sums = pl.pallas_call(
        attention_kernel,
        name="attention",
        out_shape=(
            shape((slots, width), bf16),
            shape((slots, width), f32),
            shape((moves, slots, lanes), f32),
            shape((2 * peers, 2 * slots + moves * heads, lanes), bf16),
        ),
        in_specs=[hbm] * 3 + [vmem] * 9,
        out_specs=(vmem,) * 4,
        scratch_shapes=[
            by_inst, by_move, by_move,
            pltpu.VMEM((heads, 2 * slots, HEAD), f32),
            pltpu.VMEM((slots, 2 * heads, cached), f32),
            pltpu.VMEM((2 * slots, heads, HEAD), f32),
            pltpu.VMEM((3 * slots, width), f32),
            pltpu.VMEM((slots, lanes), f32),
            pltpu.SemaphoreType.DMA((3,)),
        ],
        compiler_params=params,
    )(
        *far(move_counts, move_from, move_to),
        *near(kv_cache, ranks, first, second, parcel_other, tables, arrives, adapter, slot_lengths),
    )
    sums = lax.all_to_all(sums, ("inst", "tensor"), 0, 0, axis_index_groups=pairs)

    attn1, delta1, attn2, delta2 = pl.pallas_call(
        delta_kernel,
        name="deltas",
        out_shape=(shape((slots, width), bf16),) * 4,
        in_specs=[vmem] * 6,
        out_specs=(vmem,) * 4,
        compiler_params=params,
    )(*near(sums, tables, parcel_other, attn1, attn2_own, landing))
    return (attn1[None], delta1[None], attn2[None], delta2[None])


def solution(mesh):
    row = P("inst", None, "tensor")
    fresh = P("inst", None, None, "tensor")
    whole = P("inst", None, None, None, "tensor")
    return jax.shard_map(
        per_device,
        mesh=mesh,
        in_specs=(row, row, row, row, fresh, fresh, whole, whole, P(), P(), P(), P(), P()),
        out_specs=(row, row, row, row),
        check_vma=False,
    )
```

```python
import math

import jax
import jax.numpy as jnp
from jax import lax
from jax.experimental import pallas as pl
from jax.experimental.pallas import tpu as pltpu
from jax.sharding import PartitionSpec as P

HEAD = 128
masked_score = -1e30
f32 = jnp.float32
bf16 = jnp.bfloat16


def dot_t(a, b):
    return lax.dot_general(a, b, (((1,), (1,)), ((), ())), preferred_element_type=f32)


def dot(a, b):
    return lax.dot_general(a, b, (((1,), (0,)), ((), ())), preferred_element_type=f32)


def twice(table):
    flat = table.reshape(-1, table.shape[-1])
    return jnp.concatenate([flat, flat], 0)


def row_iota(shape):
    return lax.broadcasted_iota(jnp.int32, shape, 0)


def lane_iota(shape):
    return lax.broadcasted_iota(jnp.int32, shape, 1)


def moved_in(base, rows, arrives):
    for r in range(rows.shape[0]):
        taken = arrives[r] > 0.5
        if base.shape[1] != taken.shape[1]:
            taken = jnp.concatenate([taken] * (base.shape[1] // taken.shape[1]), 1)
        base = jnp.where(taken, rows[r : r + 1], base)
    return base


def start_all(pairs, sems, first=0):
    copies = [pltpu.make_async_copy(src, dst, sems.at[first + n]) for n, (src, dst) in enumerate(pairs)]
    for copy in copies:
        copy.start()
    return copies


def wait_all(copies):
    for copy in copies:
        copy.wait()


def halves(value):
    high = value.astype(bf16).astype(f32)
    return jnp.concatenate([high, value - high], 0)


def stage_kernel(
    ids_at, counts_at, leave_at, land_at, lengths_at, h1, h2, q1, q2, f1, f2, tables_at,
    first_out, second_out, tables_out, parcel_out, arrives_out, adapter_out, lengths_out,
    ids, counts, leave, land, lengths, fresh, fresh_wide, sems,
):
    me = lax.axis_index("inst")
    width = h1.shape[2]
    copies = start_all(
        [
            (f1.at[0], fresh.at[0]), (f2.at[0], fresh.at[1]),
            (h1.at[0], first_out.at[:, :width]), (h2.at[0], second_out.at[:, :width]),
            (q1.at[0], first_out.at[:, width : 2 * width]), (q2.at[0], second_out.at[:, width : 2 * width]),
            (ids_at, ids), (counts_at, counts), (leave_at, leave), (land_at, land), (lengths_at, lengths),
            (tables_at.at[0], tables_out),
        ],
        sems,
    )
    slots, lanes = adapter_out.shape
    rank = tables_out.shape[2]
    wait_all(copies[:2])
    fresh_wide[...] = fresh[...].astype(f32)
    for step, out in enumerate((first_out, second_out)):
        out[:, 2 * width : 2 * width + HEAD] = fresh_wide[step, :, 0, :].astype(bf16)
        out[:, 2 * width + HEAD :] = fresh_wide[step, :, 1, :].astype(bf16)
    wait_all(copies[6:11])
    row, lane = row_iota((slots, lanes)), lane_iota((slots, lanes))
    adapter = jnp.zeros((slots, lanes), jnp.int32)
    length = jnp.zeros((slots, lanes), jnp.int32)
    target = jnp.full((slots, lanes), -1, jnp.int32)
    for s in range(slots):
        adapter = jnp.where(row == s, ids[s, me], adapter)
        length = jnp.where(row == s, lengths[s, me], length)
    for m in range(leave.shape[0]):
        target = jnp.where((row == leave[m, me]) & (m < counts[me]), land[m, me], target)
    adapter_out[...] = jnp.where(lax.rem(lane, lanes // 2) // rank == adapter, 1.0, 0.0)
    lengths_out[...] = length
    for r in range(slots):
        arrives_out[r] = jnp.where(target == r, 1.0, 0.0)
    wait_all(copies[2:6] + copies[11:])
    ups = tables_out[:, 3].reshape(-1, width)
    parcel_out[: ups.shape[0]] = ups
    fresh_rows = second_out[:, 2 * width :].astype(f32)
    fresh_rows = jnp.concatenate([fresh_rows, jnp.zeros((slots, width - 2 * HEAD), f32)], 1)
    tail = jnp.concatenate([second_out[:, width : 2 * width].astype(f32), fresh_rows], 0)
    parcel_out[ups.shape[0] :] = tail.astype(bf16)


def rank_kernel(first, second, hidden_other, tables, arrives, adapter, out):
    peers, slots, lanes = out.shape
    width = tables.shape[3]
    hidden = [ref[:, :width].astype(f32) for ref in (first, second, hidden_other)]
    partials = dot_t(jnp.concatenate(hidden, 0).astype(bf16), twice(tables[:, 0]))
    moved = moved_in(partials[slots : 2 * slots], partials[2 * slots :], arrives)
    both = jnp.where(lane_iota((slots, lanes)) < lanes // 2, partials[:slots], moved)
    both = jnp.where(adapter[...] > 0.5, both, 0.0)
    for peer in range(peers):
        out[peer] = both


def attention_kernel(
    counts_at, leave_at, land_at, kv, ranks, first_rows, second_rows, parcel, tables,
    arrives, adapter, lengths,
    attn1_out, own_out, landing_out, sums_out,
    counts, leave, land, queries, scores, mixed, served_rows, rank_rows, sems,
):
    me = lax.axis_index("inst")
    half = lax.axis_size("inst") // 2
    slots, width = attn1_out.shape
    heads = width // HEAD
    cached = kv.shape[3]
    lanes = ranks.shape[2]
    moves = leave.shape[0]
    small = start_all([(counts_at, counts), (leave_at, leave), (land_at, land)], sems)

    lane = lane_iota((slots, lanes))
    low = lane < lanes // 2
    total = ranks[0]
    for peer in range(1, ranks.shape[0]):
        total = total + ranks[peer]
    total = jnp.concatenate([jnp.where(low, total, 0.0), jnp.where(low, 0.0, total)], 0).astype(bf16)
    update = dot(total, twice(tables[:, 1]))
    first = first_rows[:, width:].astype(f32)
    own = second_rows[:, width:].astype(f32)
    got = parcel[pl.ds(parcel.shape[0] - 2 * slots, 2 * slots), :].astype(f32)
    second = moved_in(own, jnp.concatenate([got[:slots], got[slots:, : 2 * HEAD]], 1), arrives)
    query1 = (first[:, :width] + update[:slots]).astype(bf16).astype(f32)
    query2 = (second[:, :width] + update[slots:]).astype(bf16).astype(f32)
    for h in range(heads):
        columns = slice(h * HEAD, (h + 1) * HEAD)
        queries[h, :slots] = query1[:, columns]
        queries[h, slots:] = query2[:, columns]
    key1, value1 = first[:, width : width + HEAD], first[:, width + HEAD :]
    key2, value2 = second[:, width : width + HEAD], second[:, width + HEAD :]

    scaling = math.log2(math.e) / math.sqrt(HEAD)
    score_shape = (2 * heads, cached)
    position = lane_iota(score_shape)
    extra = (position == cached - 2) | ((position == cached - 1) & (row_iota(score_shape) >= heads))
    last = pl.ds(cached - 16, 16)
    tail_row = row_iota((16, HEAD))

    def with_fresh(tile, one, two):
        tile = jnp.where(tail_row == 14, one, tile.astype(f32))
        return jnp.where(tail_row == 15, two, tile).astype(bf16)

    def with_tail(s, which, one, two):
        body = kv[0, s, which, : cached - 128]
        keep = kv[0, s, which, cached - 128 : cached - 16]
        return body, jnp.concatenate([keep, with_fresh(kv[0, s, which, last, :], one, two)], 0)

    for s in range(slots):
        body, tail = with_tail(s, 0, key1[s : s + 1], key2[s : s + 1])
        query = jnp.concatenate([queries[:, s, :], queries[:, slots + s, :]], 0).astype(bf16)
        score = dot_t(query, jnp.concatenate([body, tail], 0)) * scaling
        scores[s] = jnp.where((position < lengths[s : s + 1, :1]) | extra, score, masked_score)
    for s in range(slots):
        body, tail = with_tail(s, 1, value1[s : s + 1], value2[s : s + 1])
        score = scores[s]
        weights = jnp.exp2(score - jnp.max(score, 1, keepdims=True))
        probs = (weights * (1.0 / jnp.sum(weights, 1, keepdims=True))).astype(bf16)
        attended = dot(probs[:, : cached - 128], body) + dot(probs[:, cached - 128 :], tail)
        attended = attended.astype(bf16).astype(f32)
        mixed[s] = attended[:heads]
        mixed[slots + s] = attended[heads:]

    vacated = arrives[0]
    for r in range(1, slots):
        vacated = vacated + arrives[r]
    vacated = vacated > 0.5
    for h in range(heads):
        columns = slice(h * HEAD, (h + 1) * HEAD)
        served = mixed[slots:, h, :]
        served_rows[:slots, columns] = mixed[:slots, h, :]
        served_rows[slots : 2 * slots, columns] = jnp.where(vacated, own[:, width + HEAD :], served)
        served_rows[2 * slots :, columns] = served
    stacked = served_rows[...].astype(bf16)
    attn1_out[...] = served_rows[:slots].astype(bf16)
    own_out[...] = served_rows[slots : 2 * slots]

    partials = dot_t(stacked, twice(tables[:, 2]))
    mask = adapter[...] > 0.5
    for_own = jnp.where(mask, jnp.where(low, partials[:slots], partials[slots : 2 * slots]), 0.0)
    rank_rows[...] = jnp.where(mask, partials[2 * slots :], 0.0)
    for_other = jnp.zeros_like(for_own)
    row = row_iota((slots, lanes))
    wait_all(small)
    for m in range(moves):
        lands = (row == land[m, me]) & (m < counts[me])
        for_other = jnp.where(lands, rank_rows[pl.ds(leave[m, me], 1), :], for_other)
    peers = sums_out.shape[0] // 2
    lower = me < half
    for_own, for_other = halves(for_own), halves(for_other)
    in_low = jnp.where(lower, for_own, for_other).astype(bf16)
    in_high = jnp.where(lower, for_other, for_own).astype(bf16)
    sent = jnp.concatenate([mixed[slots + leave[m, me]] for m in range(moves)], 0).astype(bf16)
    for peer in range(peers):
        sums_out[peer, : 2 * slots] = in_low
        sums_out[peers + peer, : 2 * slots] = in_high
        sums_out[peer, 2 * slots :] = sent
        sums_out[peers + peer, 2 * slots :] = sent
    other = jnp.bitwise_xor(me, half)
    for m in range(moves):
        lands = (row == land[m, other]) & (m < counts[other])
        landing_out[m] = jnp.where(lands, 1.0, 0.0)


def delta_kernel(sums, tables, parcel, attn1, attn2_own, landing, attn1_out, delta1_out, attn2_out, delta2_out):
    attn1_out[...] = attn1[...]
    lower = lax.axis_index("inst") < lax.axis_size("inst") // 2
    peers = sums.shape[0] // 2
    lanes = sums.shape[2]
    slots, width = attn2_out.shape
    heads = width // HEAD
    moves = landing.shape[0]
    totals = []
    for part in range(2):
        total = sums[part * peers, : 2 * slots].astype(f32)
        for peer in range(1, peers):
            total = total + sums[part * peers + peer, : 2 * slots].astype(f32)
        totals.append(total[:slots] + total[slots:])
    own = jnp.where(lower, totals[0], totals[1])
    got = jnp.where(lower, totals[1], totals[0])
    low = lane_iota((slots, lanes)) < lanes // 2
    rank1 = jnp.where(low, own, 0.0)
    rank2_own = jnp.where(low, pltpu.roll(own, lanes // 2, 1), 0.0)
    rank2_got = jnp.where(low, 0.0, got)
    lands = [landing[m] > 0.5 for m in range(moves)]
    rank2 = rank2_own
    for m in range(moves):
        rank2 = jnp.where(lands[m], rank2_got, rank2)
    ups = tables[:, 3].reshape(-1, width)
    table = jnp.concatenate([ups, parcel[: ups.shape[0]]], 0)
    delta = dot(jnp.concatenate([rank1, rank2], 0).astype(bf16), table)
    delta1_out[...] = delta[:slots].astype(bf16)
    delta2_out[...] = delta[slots:].astype(bf16)
    sender = jnp.where(lower, peers, 0) + peers - 1 - lax.axis_index("tensor")
    moved = sums[sender, 2 * slots :, :].astype(f32)
    for h in range(heads):
        columns = slice(h * HEAD, (h + 1) * HEAD)
        rows = attn2_own[:, columns]
        for m in range(moves):
            rows = jnp.where(lands[m], moved[m * heads + h : m * heads + h + 1], rows)
        attn2_out[:, columns] = rows.astype(bf16)


def per_device(
    query_first,
    query_second,
    hidden_first,
    hidden_second,
    fresh_first,
    fresh_second,
    kv_cache,
    adapters,
    lengths,
    adapter_ids,
    move_counts,
    move_from,
    move_to,
):
    inst_count = lax.axis_size("inst")
    peers = lax.axis_size("tensor")
    half = inst_count // 2
    swap = [(i, i ^ half) for i in range(inst_count)]
    teams = [[i * peers + t for t in reversed(range(peers))] for i in range(inst_count)]
    pairs = [teams[i] + teams[i + half] for i in range(half)]
    _, slots, width = query_first.shape
    _, pool, _, rank, _ = adapters.shape
    moves = move_from.shape[1]
    lanes = 2 * pool * rank
    heads = width // HEAD
    cached = kv_cache.shape[3]
    lengths, adapter_ids, move_from, move_to = lengths.T, adapter_ids.T, move_from.T, move_to.T

    hbm = pl.BlockSpec(memory_space=pltpu.HBM)
    vmem = pl.BlockSpec(memory_space=pltpu.VMEM)
    params = pltpu.CompilerParams(vmem_limit_bytes=16 * 1024 * 1024)

    def shape(dims, dtype):
        return jax.ShapeDtypeStruct(dims, dtype)

    def far(*arrays):
        return [pltpu.with_memory_space_constraint(array, pltpu.HBM) for array in arrays]

    def near(*arrays):
        return [pltpu.with_memory_space_constraint(array, pltpu.VMEM) for array in arrays]

    by_slot = pltpu.SMEM((slots, inst_count), jnp.int32)
    by_inst = pltpu.SMEM((inst_count,), jnp.int32)
    by_move = pltpu.SMEM((moves, inst_count), jnp.int32)
    rows = shape((slots, 2 * width + 2 * HEAD), bf16)

    first, second, tables, parcel, arrives, adapter, slot_lengths = pl.pallas_call(
        stage_kernel,
        name="stage",
        out_shape=(
            rows,
            rows,
            shape(adapters.shape[1:], bf16),
            shape((pool * rank + 2 * slots, width), bf16),
            shape((slots, slots, lanes), f32),
            shape((slots, lanes), f32),
            shape((slots, lanes), jnp.int32),
        ),
        in_specs=[hbm] * 12,
        out_specs=(vmem,) * 7,
        scratch_shapes=[
            by_slot, by_inst, by_move, by_move, by_slot,
            pltpu.VMEM((2, slots, 2, HEAD), bf16),
            pltpu.VMEM((2, slots, 2, HEAD), f32),
            pltpu.SemaphoreType.DMA((12,)),
        ],
        compiler_params=params,
    )(
        *far(
            adapter_ids, move_counts, move_from, move_to, lengths,
            hidden_first, hidden_second, query_first, query_second, fresh_first, fresh_second, adapters,
        )
    )
    parcel_other = lax.ppermute(parcel, "inst", swap)
    hidden_other = lax.ppermute(hidden_second[0], "inst", swap)

    ranks = pl.pallas_call(
        rank_kernel,
        name="rank_partials",
        out_shape=shape((peers, slots, lanes), f32),
        in_specs=[vmem] * 6,
        out_specs=vmem,
        cost_estimate=pl.CostEstimate(flops=2 * 10**10, bytes_accessed=10**8, transcendentals=0),
        compiler_params=params,
    )(*near(first, second, hidden_other, tables, arrives, adapter))
    ranks = lax.all_to_all(ranks, ("inst", "tensor"), 0, 0, axis_index_groups=teams)

    attn1, attn2_own, landing, sums = pl.pallas_call(
        attention_kernel,
        name="attention",
        out_shape=(
            shape((slots, width), bf16),
            shape((slots, width), f32),
            shape((moves, slots, lanes), f32),
            shape((2 * peers, 2 * slots + moves * heads, lanes), bf16),
        ),
        in_specs=[hbm] * 3 + [vmem] * 9,
        out_specs=(vmem,) * 4,
        scratch_shapes=[
            by_inst, by_move, by_move,
            pltpu.VMEM((heads, 2 * slots, HEAD), f32),
            pltpu.VMEM((slots, 2 * heads, cached), f32),
            pltpu.VMEM((2 * slots, heads, HEAD), f32),
            pltpu.VMEM((3 * slots, width), f32),
            pltpu.VMEM((slots, lanes), f32),
            pltpu.SemaphoreType.DMA((3,)),
        ],
        compiler_params=params,
    )(
        *far(move_counts, move_from, move_to),
        *near(kv_cache, ranks, first, second, parcel_other, tables, arrives, adapter, slot_lengths),
    )
    sums = lax.all_to_all(sums, ("inst", "tensor"), 0, 0, axis_index_groups=pairs)

    attn1, delta1, attn2, delta2 = pl.pallas_call(
        delta_kernel,
        name="deltas",
        out_shape=(shape((slots, width), bf16),) * 4,
        in_specs=[vmem] * 6,
        out_specs=(vmem,) * 4,
        compiler_params=params,
    )(*near(sums, tables, parcel_other, attn1, attn2_own, landing))
    return (attn1[None], delta1[None], attn2[None], delta2[None])


def solution(mesh):
    row = P("inst", None, "tensor")
    fresh = P("inst", None, None, "tensor")
    whole = P("inst", None, None, None, "tensor")
    return jax.shard_map(
        per_device,
        mesh=mesh,
        in_specs=(row, row, row, row, fresh, fresh, whole, whole, P(), P(), P(), P(), P()),
        out_specs=(row, row, row, row),
        check_vma=False,
    )
```

```python
import math

import jax
import jax.numpy as jnp
from jax import lax
from jax.experimental import pallas as pl
from jax.experimental.pallas import tpu as pltpu
from jax.sharding import PartitionSpec as P

HEAD = 128
masked_score = -1e30
f32 = jnp.float32
bf16 = jnp.bfloat16


def dot_t(a, b):
    return lax.dot_general(a, b, (((1,), (1,)), ((), ())), preferred_element_type=f32)


def dot(a, b):
    return lax.dot_general(a, b, (((1,), (0,)), ((), ())), preferred_element_type=f32)


def twice(table):
    flat = table.reshape(-1, table.shape[-1])
    return jnp.concatenate([flat, flat], 0)


def row_iota(shape):
    return lax.broadcasted_iota(jnp.int32, shape, 0)


def lane_iota(shape):
    return lax.broadcasted_iota(jnp.int32, shape, 1)


def moved_in(base, rows, arrives):
    for r in range(rows.shape[0]):
        taken = arrives[r] > 0.5
        if base.shape[1] != taken.shape[1]:
            taken = jnp.concatenate([taken] * (base.shape[1] // taken.shape[1]), 1)
        base = jnp.where(taken, rows[r : r + 1], base)
    return base


def start_all(pairs, sems, first=0):
    copies = [pltpu.make_async_copy(src, dst, sems.at[first + n]) for n, (src, dst) in enumerate(pairs)]
    for copy in copies:
        copy.start()
    return copies


def wait_all(copies):
    for copy in copies:
        copy.wait()


def halves(value):
    high = value.astype(bf16).astype(f32)
    return jnp.concatenate([high, value - high], 0)


def stage_kernel(
    ids_at, counts_at, leave_at, land_at, lengths_at, h1, h2, q1, q2, f1, f2, tables_at,
    first_out, second_out, down_out, parcel_out, arrives_out, adapter_out, lengths_out,
    ids, counts, leave, land, lengths, fresh, fresh_wide, up, sems,
):
    me = lax.axis_index("inst")
    width = h1.shape[2]
    copies = start_all(
        [
            (f1.at[0], fresh.at[0]), (f2.at[0], fresh.at[1]),
            (h1.at[0], first_out.at[:, :width]), (h2.at[0], second_out.at[:, :width]),
            (q1.at[0], first_out.at[:, width : 2 * width]), (q2.at[0], second_out.at[:, width : 2 * width]),
            (ids_at, ids), (counts_at, counts), (leave_at, leave), (land_at, land), (lengths_at, lengths),
            (tables_at.at[0, :, 0], down_out), (tables_at.at[0, :, 3], up),
        ],
        sems,
    )
    slots, lanes = adapter_out.shape
    rank = down_out.shape[1]
    wait_all(copies[:2])
    fresh_wide[...] = fresh[...].astype(f32)
    for step, out in enumerate((first_out, second_out)):
        out[:, 2 * width : 2 * width + HEAD] = fresh_wide[step, :, 0, :].astype(bf16)
        out[:, 2 * width + HEAD :] = fresh_wide[step, :, 1, :].astype(bf16)
    wait_all(copies[6:11])
    row, lane = row_iota((slots, lanes)), lane_iota((slots, lanes))
    adapter = jnp.zeros((slots, lanes), jnp.int32)
    length = jnp.zeros((slots, lanes), jnp.int32)
    target = jnp.full((slots, lanes), -1, jnp.int32)
    for s in range(slots):
        adapter = jnp.where(row == s, ids[s, me], adapter)
        length = jnp.where(row == s, lengths[s, me], length)
    for m in range(leave.shape[0]):
        target = jnp.where((row == leave[m, me]) & (m < counts[me]), land[m, me], target)
    adapter_out[...] = jnp.where(lax.rem(lane, lanes // 2) // rank == adapter, 1.0, 0.0)
    lengths_out[...] = length
    for r in range(slots):
        arrives_out[r] = jnp.where(target == r, 1.0, 0.0)
    wait_all(copies[2:6] + copies[11:])
    ups = up[...].reshape(-1, width)
    parcel_out[: ups.shape[0]] = ups
    fresh_rows = second_out[:, 2 * width :].astype(f32)
    fresh_rows = jnp.concatenate([fresh_rows, jnp.zeros((slots, width - 2 * HEAD), f32)], 1)
    tail = jnp.concatenate([second_out[:, width : 2 * width].astype(f32), fresh_rows], 0)
    parcel_out[ups.shape[0] :] = tail.astype(bf16)


def rank_kernel(first, second, hidden_other, down, arrives, adapter, out):
    peers, slots, lanes = out.shape
    width = down.shape[2]
    hidden = [ref[:, :width].astype(f32) for ref in (first, second, hidden_other)]
    partials = dot_t(jnp.concatenate(hidden, 0).astype(bf16), twice(down[...]))
    moved = moved_in(partials[slots : 2 * slots], partials[2 * slots :], arrives)
    both = jnp.where(lane_iota((slots, lanes)) < lanes // 2, partials[:slots], moved)
    both = jnp.where(adapter[...] > 0.5, both, 0.0)
    for peer in range(peers):
        out[peer] = both


def attention_kernel(
    counts_at, leave_at, land_at, kv, ranks, first_rows, second_rows, parcel, tables,
    arrives, adapter, lengths,
    attn1_out, own_out, landing_out, sums_out,
    counts, leave, land, queries, scores, mixed, served_rows, rank_rows, sems,
):
    me = lax.axis_index("inst")
    half = lax.axis_size("inst") // 2
    slots, width = attn1_out.shape
    heads = width // HEAD
    cached = kv.shape[3]
    lanes = ranks.shape[2]
    moves = leave.shape[0]
    small = start_all([(counts_at, counts), (leave_at, leave), (land_at, land)], sems)

    lane = lane_iota((slots, lanes))
    low = lane < lanes // 2
    total = ranks[0]
    for peer in range(1, ranks.shape[0]):
        total = total + ranks[peer]
    total = jnp.concatenate([jnp.where(low, total, 0.0), jnp.where(low, 0.0, total)], 0).astype(bf16)
    update = dot(total, twice(tables[0, :, 1]))
    first = first_rows[:, width:].astype(f32)
    own = second_rows[:, width:].astype(f32)
    got = parcel[pl.ds(parcel.shape[0] - 2 * slots, 2 * slots), :].astype(f32)
    second = moved_in(own, jnp.concatenate([got[:slots], got[slots:, : 2 * HEAD]], 1), arrives)
    query1 = (first[:, :width] + update[:slots]).astype(bf16).astype(f32)
    query2 = (second[:, :width] + update[slots:]).astype(bf16).astype(f32)
    for h in range(heads):
        columns = slice(h * HEAD, (h + 1) * HEAD)
        queries[h, :slots] = query1[:, columns]
        queries[h, slots:] = query2[:, columns]
    key1, value1 = first[:, width : width + HEAD], first[:, width + HEAD :]
    key2, value2 = second[:, width : width + HEAD], second[:, width + HEAD :]

    scaling = math.log2(math.e) / math.sqrt(HEAD)
    score_shape = (2 * heads, cached)
    position = lane_iota(score_shape)
    extra = (position == cached - 2) | ((position == cached - 1) & (row_iota(score_shape) >= heads))
    last = pl.ds(cached - 16, 16)
    tail_row = row_iota((16, HEAD))

    def with_fresh(tile, one, two):
        tile = jnp.where(tail_row == 14, one, tile.astype(f32))
        return jnp.where(tail_row == 15, two, tile).astype(bf16)

    def with_tail(s, which, one, two):
        body = kv[0, s, which, : cached - 128]
        keep = kv[0, s, which, cached - 128 : cached - 16]
        return body, jnp.concatenate([keep, with_fresh(kv[0, s, which, last, :], one, two)], 0)

    for s in range(slots):
        body, tail = with_tail(s, 0, key1[s : s + 1], key2[s : s + 1])
        query = jnp.concatenate([queries[:, s, :], queries[:, slots + s, :]], 0).astype(bf16)
        score = dot_t(query, jnp.concatenate([body, tail], 0)) * scaling
        scores[s] = jnp.where((position < lengths[s : s + 1, :1]) | extra, score, masked_score)
    for s in range(slots):
        body, tail = with_tail(s, 1, value1[s : s + 1], value2[s : s + 1])
        score = scores[s]
        weights = jnp.exp2(score - jnp.max(score, 1, keepdims=True))
        probs = (weights * (1.0 / jnp.sum(weights, 1, keepdims=True))).astype(bf16)
        attended = dot(probs[:, : cached - 128], body) + dot(probs[:, cached - 128 :], tail)
        attended = attended.astype(bf16).astype(f32)
        mixed[s] = attended[:heads]
        mixed[slots + s] = attended[heads:]

    vacated = arrives[0]
    for r in range(1, slots):
        vacated = vacated + arrives[r]
    vacated = vacated > 0.5
    for h in range(heads):
        columns = slice(h * HEAD, (h + 1) * HEAD)
        served = mixed[slots:, h, :]
        served_rows[:slots, columns] = mixed[:slots, h, :]
        served_rows[slots : 2 * slots, columns] = jnp.where(vacated, own[:, width + HEAD :], served)
        served_rows[2 * slots :, columns] = served
    stacked = served_rows[...].astype(bf16)
    attn1_out[...] = served_rows[:slots].astype(bf16)
    own_out[...] = served_rows[slots : 2 * slots]

    partials = dot_t(stacked, twice(tables[0, :, 2]))
    mask = adapter[...] > 0.5
    for_own = jnp.where(mask, jnp.where(low, partials[:slots], partials[slots : 2 * slots]), 0.0)
    rank_rows[...] = jnp.where(mask, partials[2 * slots :], 0.0)
    for_other = jnp.zeros_like(for_own)
    row = row_iota((slots, lanes))
    wait_all(small)
    for m in range(moves):
        lands = (row == land[m, me]) & (m < counts[me])
        for_other = jnp.where(lands, rank_rows[pl.ds(leave[m, me], 1), :], for_other)
    peers = sums_out.shape[0] // 2
    lower = me < half
    for_own, for_other = halves(for_own), halves(for_other)
    in_low = jnp.where(lower, for_own, for_other).astype(bf16)
    in_high = jnp.where(lower, for_other, for_own).astype(bf16)
    sent = jnp.concatenate([mixed[slots + leave[m, me]] for m in range(moves)], 0).astype(bf16)
    for peer in range(peers):
        sums_out[peer, : 2 * slots] = in_low
        sums_out[peers + peer, : 2 * slots] = in_high
        sums_out[peer, 2 * slots :] = sent
        sums_out[peers + peer, 2 * slots :] = sent
    other = jnp.bitwise_xor(me, half)
    for m in range(moves):
        lands = (row == land[m, other]) & (m < counts[other])
        landing_out[m] = jnp.where(lands, 1.0, 0.0)


def delta_kernel(sums, tables, parcel, attn1, attn2_own, landing, attn1_out, delta1_out, attn2_out, delta2_out):
    attn1_out[...] = attn1[...]
    lower = lax.axis_index("inst") < lax.axis_size("inst") // 2
    peers = sums.shape[0] // 2
    lanes = sums.shape[2]
    slots, width = attn2_out.shape
    heads = width // HEAD
    moves = landing.shape[0]
    totals = []
    for part in range(2):
        total = sums[part * peers, : 2 * slots].astype(f32)
        for peer in range(1, peers):
            total = total + sums[part * peers + peer, : 2 * slots].astype(f32)
        totals.append(total[:slots] + total[slots:])
    own = jnp.where(lower, totals[0], totals[1])
    got = jnp.where(lower, totals[1], totals[0])
    low = lane_iota((slots, lanes)) < lanes // 2
    rank1 = jnp.where(low, own, 0.0)
    rank2_own = jnp.where(low, pltpu.roll(own, lanes // 2, 1), 0.0)
    rank2_got = jnp.where(low, 0.0, got)
    lands = [landing[m] > 0.5 for m in range(moves)]
    rank2 = rank2_own
    for m in range(moves):
        rank2 = jnp.where(lands[m], rank2_got, rank2)
    ups = tables[0, :, 3].reshape(-1, width)
    table = jnp.concatenate([ups, parcel[: ups.shape[0]]], 0)
    delta = dot(jnp.concatenate([rank1, rank2], 0).astype(bf16), table)
    delta1_out[...] = delta[:slots].astype(bf16)
    delta2_out[...] = delta[slots:].astype(bf16)
    sender = jnp.where(lower, peers, 0) + peers - 1 - lax.axis_index("tensor")
    moved = sums[sender, 2 * slots :, :].astype(f32)
    for h in range(heads):
        columns = slice(h * HEAD, (h + 1) * HEAD)
        rows = attn2_own[:, columns]
        for m in range(moves):
            rows = jnp.where(lands[m], moved[m * heads + h : m * heads + h + 1], rows)
        attn2_out[:, columns] = rows.astype(bf16)


def per_device(
    query_first,
    query_second,
    hidden_first,
    hidden_second,
    fresh_first,
    fresh_second,
    kv_cache,
    adapters,
    lengths,
    adapter_ids,
    move_counts,
    move_from,
    move_to,
):
    inst_count = lax.axis_size("inst")
    peers = lax.axis_size("tensor")
    half = inst_count // 2
    swap = [(i, i ^ half) for i in range(inst_count)]
    teams = [[i * peers + t for t in reversed(range(peers))] for i in range(inst_count)]
    pairs = [teams[i] + teams[i + half] for i in range(half)]
    _, slots, width = query_first.shape
    _, pool, _, rank, _ = adapters.shape
    moves = move_from.shape[1]
    lanes = 2 * pool * rank
    heads = width // HEAD
    cached = kv_cache.shape[3]
    lengths, adapter_ids, move_from, move_to = lengths.T, adapter_ids.T, move_from.T, move_to.T

    hbm = pl.BlockSpec(memory_space=pltpu.HBM)
    vmem = pl.BlockSpec(memory_space=pltpu.VMEM)
    params = pltpu.CompilerParams(vmem_limit_bytes=16 * 1024 * 1024)

    def shape(dims, dtype):
        return jax.ShapeDtypeStruct(dims, dtype)

    def far(*arrays):
        return [pltpu.with_memory_space_constraint(array, pltpu.HBM) for array in arrays]

    def near(*arrays):
        return [pltpu.with_memory_space_constraint(array, pltpu.VMEM) for array in arrays]

    by_slot = pltpu.SMEM((slots, inst_count), jnp.int32)
    by_inst = pltpu.SMEM((inst_count,), jnp.int32)
    by_move = pltpu.SMEM((moves, inst_count), jnp.int32)
    rows = shape((slots, 2 * width + 2 * HEAD), bf16)

    first, second, down, parcel, arrives, adapter, slot_lengths = pl.pallas_call(
        stage_kernel,
        name="stage",
        out_shape=(
            rows,
            rows,
            shape((pool, rank, width), bf16),
            shape((pool * rank + 2 * slots, width), bf16),
            shape((slots, slots, lanes), f32),
            shape((slots, lanes), f32),
            shape((slots, lanes), jnp.int32),
        ),
        in_specs=[hbm] * 12,
        out_specs=(vmem,) * 7,
        scratch_shapes=[
            by_slot, by_inst, by_move, by_move, by_slot,
            pltpu.VMEM((2, slots, 2, HEAD), bf16),
            pltpu.VMEM((2, slots, 2, HEAD), f32),
            pltpu.VMEM((pool, rank, width), bf16),
            pltpu.SemaphoreType.DMA((13,)),
        ],
        compiler_params=params,
    )(
        *far(
            adapter_ids, move_counts, move_from, move_to, lengths,
            hidden_first, hidden_second, query_first, query_second, fresh_first, fresh_second, adapters,
        )
    )
    parcel_other = lax.ppermute(parcel, "inst", swap)
    hidden_other = lax.ppermute(hidden_second[0], "inst", swap)

    ranks = pl.pallas_call(
        rank_kernel,
        name="rank_partials",
        out_shape=shape((peers, slots, lanes), f32),
        in_specs=[vmem] * 6,
        out_specs=vmem,
        cost_estimate=pl.CostEstimate(flops=2 * 10**10, bytes_accessed=10**8, transcendentals=0),
        compiler_params=params,
    )(*near(first, second, hidden_other, down, arrives, adapter))
    ranks = lax.all_to_all(ranks, ("inst", "tensor"), 0, 0, axis_index_groups=teams)

    attn1, attn2_own, landing, sums = pl.pallas_call(
        attention_kernel,
        name="attention",
        out_shape=(
            shape((slots, width), bf16),
            shape((slots, width), f32),
            shape((moves, slots, lanes), f32),
            shape((2 * peers, 2 * slots + moves * heads, lanes), bf16),
        ),
        in_specs=[hbm] * 3 + [vmem] * 9,
        out_specs=(vmem,) * 4,
        scratch_shapes=[
            by_inst, by_move, by_move,
            pltpu.VMEM((heads, 2 * slots, HEAD), f32),
            pltpu.VMEM((slots, 2 * heads, cached), f32),
            pltpu.VMEM((2 * slots, heads, HEAD), f32),
            pltpu.VMEM((3 * slots, width), f32),
            pltpu.VMEM((slots, lanes), f32),
            pltpu.SemaphoreType.DMA((3,)),
        ],
        compiler_params=params,
    )(
        *far(move_counts, move_from, move_to),
        *near(kv_cache, ranks, first, second, parcel_other, adapters, arrives, adapter, slot_lengths),
    )
    sums = lax.all_to_all(sums, ("inst", "tensor"), 0, 0, axis_index_groups=pairs)

    attn1, delta1, attn2, delta2 = pl.pallas_call(
        delta_kernel,
        name="deltas",
        out_shape=(shape((slots, width), bf16),) * 4,
        in_specs=[vmem] * 6,
        out_specs=(vmem,) * 4,
        compiler_params=params,
    )(*near(sums, adapters, parcel_other, attn1, attn2_own, landing))
    return (attn1[None], delta1[None], attn2[None], delta2[None])


def solution(mesh):
    row = P("inst", None, "tensor")
    fresh = P("inst", None, None, "tensor")
    whole = P("inst", None, None, None, "tensor")
    return jax.shard_map(
        per_device,
        mesh=mesh,
        in_specs=(row, row, row, row, fresh, fresh, whole, whole, P(), P(), P(), P(), P()),
        out_specs=(row, row, row, row),
        check_vma=False,
    )
```

```python
import math

import jax
import jax.numpy as jnp
from jax import lax
from jax.experimental import pallas as pl
from jax.experimental.pallas import tpu as pltpu
from jax.sharding import PartitionSpec as P

HEAD = 128
masked_score = -1e30
f32 = jnp.float32
bf16 = jnp.bfloat16


def dot_t(a, b):
    return lax.dot_general(a, b, (((1,), (1,)), ((), ())), preferred_element_type=f32)


def dot(a, b):
    return lax.dot_general(a, b, (((1,), (0,)), ((), ())), preferred_element_type=f32)


def twice(table):
    flat = table.reshape(-1, table.shape[-1])
    return jnp.concatenate([flat, flat], 0)


def row_iota(shape):
    return lax.broadcasted_iota(jnp.int32, shape, 0)


def lane_iota(shape):
    return lax.broadcasted_iota(jnp.int32, shape, 1)


def moved_in(base, rows, arrives):
    for r in range(rows.shape[0]):
        taken = arrives[r] > 0.5
        if base.shape[1] != taken.shape[1]:
            taken = jnp.concatenate([taken] * (base.shape[1] // taken.shape[1]), 1)
        base = jnp.where(taken, rows[r : r + 1], base)
    return base


def start_all(pairs, sems, first=0):
    copies = [pltpu.make_async_copy(src, dst, sems.at[first + n]) for n, (src, dst) in enumerate(pairs)]
    for copy in copies:
        copy.start()
    return copies


def wait_all(copies):
    for copy in copies:
        copy.wait()


def halves(value):
    high = value.astype(bf16).astype(f32)
    return jnp.concatenate([high, value - high], 0)


def stage_kernel(
    ids_at, counts_at, leave_at, land_at, lengths_at, h1, h2, q2, f2, tables_at,
    first_out, second_out, down_out, parcel_out, arrives_out, adapter_out, lengths_out,
    ids, counts, leave, land, lengths, fresh, fresh_wide, up, sems,
):
    me = lax.axis_index("inst")
    width = h1.shape[2]
    copies = start_all(
        [
            (f2.at[0], fresh), (h1.at[0], first_out),
            (h2.at[0], second_out.at[:, :width]), (q2.at[0], second_out.at[:, width : 2 * width]),
            (ids_at, ids), (counts_at, counts), (leave_at, leave), (land_at, land), (lengths_at, lengths),
            (tables_at.at[0, :, 0], down_out), (tables_at.at[0, :, 3], up),
        ],
        sems,
    )
    slots, lanes = adapter_out.shape
    rank = down_out.shape[1]
    wait_all(copies[:1])
    fresh_wide[...] = fresh[...].astype(f32)
    second_out[:, 2 * width : 2 * width + HEAD] = fresh_wide[:, 0, :].astype(bf16)
    second_out[:, 2 * width + HEAD :] = fresh_wide[:, 1, :].astype(bf16)
    wait_all(copies[4:9])
    row, lane = row_iota((slots, lanes)), lane_iota((slots, lanes))
    adapter = jnp.zeros((slots, lanes), jnp.int32)
    length = jnp.zeros((slots, lanes), jnp.int32)
    target = jnp.full((slots, lanes), -1, jnp.int32)
    for s in range(slots):
        adapter = jnp.where(row == s, ids[s, me], adapter)
        length = jnp.where(row == s, lengths[s, me], length)
    for m in range(leave.shape[0]):
        target = jnp.where((row == leave[m, me]) & (m < counts[me]), land[m, me], target)
    adapter_out[...] = jnp.where(lax.rem(lane, lanes // 2) // rank == adapter, 1.0, 0.0)
    lengths_out[...] = length
    for r in range(slots):
        arrives_out[r] = jnp.where(target == r, 1.0, 0.0)
    wait_all(copies[1:4] + copies[9:])
    ups = up[...].reshape(-1, width)
    parcel_out[: ups.shape[0]] = ups
    fresh_rows = second_out[:, 2 * width :].astype(f32)
    fresh_rows = jnp.concatenate([fresh_rows, jnp.zeros((slots, width - 2 * HEAD), f32)], 1)
    tail = jnp.concatenate([second_out[:, width : 2 * width].astype(f32), fresh_rows], 0)
    parcel_out[ups.shape[0] :] = tail.astype(bf16)


def rank_kernel(first, second, hidden_other, down, arrives, adapter, out):
    peers, slots, lanes = out.shape
    width = down.shape[2]
    hidden = [ref[:, :width].astype(f32) for ref in (first, second, hidden_other)]
    partials = dot_t(jnp.concatenate(hidden, 0).astype(bf16), twice(down[...]))
    moved = moved_in(partials[slots : 2 * slots], partials[2 * slots :], arrives)
    both = jnp.where(lane_iota((slots, lanes)) < lanes // 2, partials[:slots], moved)
    both = jnp.where(adapter[...] > 0.5, both, 0.0)
    for peer in range(peers):
        out[peer] = both


def attention_kernel(
    counts_at, leave_at, land_at, kv, ranks, base1, fresh1, second_rows, parcel, tables,
    arrives, adapter, lengths,
    attn1_out, own_out, landing_out, sums_out,
    counts, leave, land, queries, scores, mixed, served_rows, rank_rows, fresh_wide, sems,
):
    me = lax.axis_index("inst")
    half = lax.axis_size("inst") // 2
    slots, width = attn1_out.shape
    heads = width // HEAD
    cached = kv.shape[3]
    lanes = ranks.shape[2]
    moves = leave.shape[0]
    small = start_all([(counts_at, counts), (leave_at, leave), (land_at, land)], sems)

    lane = lane_iota((slots, lanes))
    low = lane < lanes // 2
    total = ranks[0]
    for peer in range(1, ranks.shape[0]):
        total = total + ranks[peer]
    total = jnp.concatenate([jnp.where(low, total, 0.0), jnp.where(low, 0.0, total)], 0).astype(bf16)
    update = dot(total, twice(tables[0, :, 1]))
    fresh_wide[...] = fresh1[0].astype(f32)
    own = second_rows[:, width:].astype(f32)
    got = parcel[pl.ds(parcel.shape[0] - 2 * slots, 2 * slots), :].astype(f32)
    second = moved_in(own, jnp.concatenate([got[:slots], got[slots:, : 2 * HEAD]], 1), arrives)
    query1 = (base1[0].astype(f32) + update[:slots]).astype(bf16).astype(f32)
    query2 = (second[:, :width] + update[slots:]).astype(bf16).astype(f32)
    for h in range(heads):
        columns = slice(h * HEAD, (h + 1) * HEAD)
        queries[h, :slots] = query1[:, columns]
        queries[h, slots:] = query2[:, columns]
    key1, value1 = fresh_wide[:, 0, :], fresh_wide[:, 1, :]
    key2, value2 = second[:, width : width + HEAD], second[:, width + HEAD :]

    scaling = math.log2(math.e) / math.sqrt(HEAD)
    score_shape = (2 * heads, cached)
    position = lane_iota(score_shape)
    extra = (position == cached - 2) | ((position == cached - 1) & (row_iota(score_shape) >= heads))
    last = pl.ds(cached - 16, 16)
    tail_row = row_iota((16, HEAD))

    def with_fresh(tile, one, two):
        tile = jnp.where(tail_row == 14, one, tile.astype(f32))
        return jnp.where(tail_row == 15, two, tile).astype(bf16)

    def with_tail(s, which, one, two):
        body = kv[0, s, which, : cached - 128]
        keep = kv[0, s, which, cached - 128 : cached - 16]
        return body, jnp.concatenate([keep, with_fresh(kv[0, s, which, last, :], one, two)], 0)

    for s in range(slots):
        body, tail = with_tail(s, 0, key1[s : s + 1], key2[s : s + 1])
        query = jnp.concatenate([queries[:, s, :], queries[:, slots + s, :]], 0).astype(bf16)
        score = dot_t(query, jnp.concatenate([body, tail], 0)) * scaling
        scores[s] = jnp.where((position < lengths[s : s + 1, :1]) | extra, score, masked_score)
    for s in range(slots):
        body, tail = with_tail(s, 1, value1[s : s + 1], value2[s : s + 1])
        score = scores[s]
        weights = jnp.exp2(score - jnp.max(score, 1, keepdims=True))
        probs = (weights * (1.0 / jnp.sum(weights, 1, keepdims=True))).astype(bf16)
        attended = dot(probs[:, : cached - 128], body) + dot(probs[:, cached - 128 :], tail)
        attended = attended.astype(bf16).astype(f32)
        mixed[s] = attended[:heads]
        mixed[slots + s] = attended[heads:]

    vacated = arrives[0]
    for r in range(1, slots):
        vacated = vacated + arrives[r]
    vacated = vacated > 0.5
    for h in range(heads):
        columns = slice(h * HEAD, (h + 1) * HEAD)
        served = mixed[slots:, h, :]
        served_rows[:slots, columns] = mixed[:slots, h, :]
        served_rows[slots : 2 * slots, columns] = jnp.where(vacated, own[:, width + HEAD :], served)
        served_rows[2 * slots :, columns] = served
    stacked = served_rows[...].astype(bf16)
    attn1_out[...] = served_rows[:slots].astype(bf16)
    own_out[...] = served_rows[slots : 2 * slots]

    partials = dot_t(stacked, twice(tables[0, :, 2]))
    mask = adapter[...] > 0.5
    for_own = jnp.where(mask, jnp.where(low, partials[:slots], partials[slots : 2 * slots]), 0.0)
    rank_rows[...] = jnp.where(mask, partials[2 * slots :], 0.0)
    for_other = jnp.zeros_like(for_own)
    row = row_iota((slots, lanes))
    wait_all(small)
    for m in range(moves):
        lands = (row == land[m, me]) & (m < counts[me])
        for_other = jnp.where(lands, rank_rows[pl.ds(leave[m, me], 1), :], for_other)
    peers = sums_out.shape[0] // 2
    lower = me < half
    for_own, for_other = halves(for_own), halves(for_other)
    in_low = jnp.where(lower, for_own, for_other).astype(bf16)
    in_high = jnp.where(lower, for_other, for_own).astype(bf16)
    sent = jnp.concatenate([mixed[slots + leave[m, me]] for m in range(moves)], 0).astype(bf16)
    for peer in range(peers):
        sums_out[peer, : 2 * slots] = in_low
        sums_out[peers + peer, : 2 * slots] = in_high
        sums_out[peer, 2 * slots :] = sent
        sums_out[peers + peer, 2 * slots :] = sent
    other = jnp.bitwise_xor(me, half)
    for m in range(moves):
        lands = (row == land[m, other]) & (m < counts[other])
        landing_out[m] = jnp.where(lands, 1.0, 0.0)


def delta_kernel(sums, tables, parcel, attn1, attn2_own, landing, attn1_out, delta1_out, attn2_out, delta2_out):
    attn1_out[...] = attn1[...]
    lower = lax.axis_index("inst") < lax.axis_size("inst") // 2
    peers = sums.shape[0] // 2
    lanes = sums.shape[2]
    slots, width = attn2_out.shape
    heads = width // HEAD
    moves = landing.shape[0]
    totals = []
    for part in range(2):
        total = sums[part * peers, : 2 * slots].astype(f32)
        for peer in range(1, peers):
            total = total + sums[part * peers + peer, : 2 * slots].astype(f32)
        totals.append(total[:slots] + total[slots:])
    own = jnp.where(lower, totals[0], totals[1])
    got = jnp.where(lower, totals[1], totals[0])
    low = lane_iota((slots, lanes)) < lanes // 2
    rank1 = jnp.where(low, own, 0.0)
    rank2_own = jnp.where(low, pltpu.roll(own, lanes // 2, 1), 0.0)
    rank2_got = jnp.where(low, 0.0, got)
    lands = [landing[m] > 0.5 for m in range(moves)]
    rank2 = rank2_own
    for m in range(moves):
        rank2 = jnp.where(lands[m], rank2_got, rank2)
    ups = tables[0, :, 3].reshape(-1, width)
    table = jnp.concatenate([ups, parcel[: ups.shape[0]]], 0)
    delta = dot(jnp.concatenate([rank1, rank2], 0).astype(bf16), table)
    delta1_out[...] = delta[:slots].astype(bf16)
    delta2_out[...] = delta[slots:].astype(bf16)
    sender = jnp.where(lower, peers, 0) + peers - 1 - lax.axis_index("tensor")
    moved = sums[sender, 2 * slots :, :].astype(f32)
    for h in range(heads):
        columns = slice(h * HEAD, (h + 1) * HEAD)
        rows = attn2_own[:, columns]
        for m in range(moves):
            rows = jnp.where(lands[m], moved[m * heads + h : m * heads + h + 1], rows)
        attn2_out[:, columns] = rows.astype(bf16)


def per_device(
    query_first,
    query_second,
    hidden_first,
    hidden_second,
    fresh_first,
    fresh_second,
    kv_cache,
    adapters,
    lengths,
    adapter_ids,
    move_counts,
    move_from,
    move_to,
):
    inst_count = lax.axis_size("inst")
    peers = lax.axis_size("tensor")
    half = inst_count // 2
    swap = [(i, i ^ half) for i in range(inst_count)]
    teams = [[i * peers + t for t in reversed(range(peers))] for i in range(inst_count)]
    pairs = [teams[i] + teams[i + half] for i in range(half)]
    _, slots, width = query_first.shape
    _, pool, _, rank, _ = adapters.shape
    moves = move_from.shape[1]
    lanes = 2 * pool * rank
    heads = width // HEAD
    cached = kv_cache.shape[3]
    lengths, adapter_ids, move_from, move_to = lengths.T, adapter_ids.T, move_from.T, move_to.T

    hbm = pl.BlockSpec(memory_space=pltpu.HBM)
    vmem = pl.BlockSpec(memory_space=pltpu.VMEM)
    params = pltpu.CompilerParams(vmem_limit_bytes=16 * 1024 * 1024)

    def shape(dims, dtype):
        return jax.ShapeDtypeStruct(dims, dtype)

    def far(*arrays):
        return [pltpu.with_memory_space_constraint(array, pltpu.HBM) for array in arrays]

    def near(*arrays):
        return [pltpu.with_memory_space_constraint(array, pltpu.VMEM) for array in arrays]

    by_slot = pltpu.SMEM((slots, inst_count), jnp.int32)
    by_inst = pltpu.SMEM((inst_count,), jnp.int32)
    by_move = pltpu.SMEM((moves, inst_count), jnp.int32)
    rows = shape((slots, 2 * width + 2 * HEAD), bf16)

    first, second, down, parcel, arrives, adapter, slot_lengths = pl.pallas_call(
        stage_kernel,
        name="stage",
        out_shape=(
            shape((slots, width), bf16),
            rows,
            shape((pool, rank, width), bf16),
            shape((pool * rank + 2 * slots, width), bf16),
            shape((slots, slots, lanes), f32),
            shape((slots, lanes), f32),
            shape((slots, lanes), jnp.int32),
        ),
        in_specs=[hbm] * 10,
        out_specs=(vmem,) * 7,
        scratch_shapes=[
            by_slot, by_inst, by_move, by_move, by_slot,
            pltpu.VMEM((slots, 2, HEAD), bf16),
            pltpu.VMEM((slots, 2, HEAD), f32),
            pltpu.VMEM((pool, rank, width), bf16),
            pltpu.SemaphoreType.DMA((11,)),
        ],
        compiler_params=params,
    )(
        *far(
            adapter_ids, move_counts, move_from, move_to, lengths,
            hidden_first, hidden_second, query_second, fresh_second, adapters,
        )
    )
    parcel_other = lax.ppermute(parcel, "inst", swap)
    hidden_other = lax.ppermute(hidden_second[0], "inst", swap)

    ranks = pl.pallas_call(
        rank_kernel,
        name="rank_partials",
        out_shape=shape((peers, slots, lanes), f32),
        in_specs=[vmem] * 6,
        out_specs=vmem,
        cost_estimate=pl.CostEstimate(flops=2 * 10**10, bytes_accessed=10**8, transcendentals=0),
        compiler_params=params,
    )(*near(first, second, hidden_other, down, arrives, adapter))
    ranks = lax.all_to_all(ranks, ("inst", "tensor"), 0, 0, axis_index_groups=teams)

    attn1, attn2_own, landing, sums = pl.pallas_call(
        attention_kernel,
        name="attention",
        out_shape=(
            shape((slots, width), bf16),
            shape((slots, width), f32),
            shape((moves, slots, lanes), f32),
            shape((2 * peers, 2 * slots + moves * heads, lanes), bf16),
        ),
        in_specs=[hbm] * 3 + [vmem] * 10,
        out_specs=(vmem,) * 4,
        scratch_shapes=[
            by_inst, by_move, by_move,
            pltpu.VMEM((heads, 2 * slots, HEAD), f32),
            pltpu.VMEM((slots, 2 * heads, cached), f32),
            pltpu.VMEM((2 * slots, heads, HEAD), f32),
            pltpu.VMEM((3 * slots, width), f32),
            pltpu.VMEM((slots, lanes), f32),
            pltpu.VMEM((slots, 2, HEAD), f32),
            pltpu.SemaphoreType.DMA((3,)),
        ],
        compiler_params=params,
    )(
        *far(move_counts, move_from, move_to),
        *near(kv_cache, ranks, query_first, fresh_first, second, parcel_other, adapters, arrives, adapter, slot_lengths),
    )
    sums = lax.all_to_all(sums, ("inst", "tensor"), 0, 0, axis_index_groups=pairs)

    attn1, delta1, attn2, delta2 = pl.pallas_call(
        delta_kernel,
        name="deltas",
        out_shape=(shape((slots, width), bf16),) * 4,
        in_specs=[vmem] * 6,
        out_specs=(vmem,) * 4,
        compiler_params=params,
    )(*near(sums, adapters, parcel_other, attn1, attn2_own, landing))
    return (attn1[None], delta1[None], attn2[None], delta2[None])


def solution(mesh):
    row = P("inst", None, "tensor")
    fresh = P("inst", None, None, "tensor")
    whole = P("inst", None, None, None, "tensor")
    return jax.shard_map(
        per_device,
        mesh=mesh,
        in_specs=(row, row, row, row, fresh, fresh, whole, whole, P(), P(), P(), P(), P()),
        out_specs=(row, row, row, row),
        check_vma=False,
    )
```

```python
import math

import jax
import jax.numpy as jnp
from jax import lax
from jax.experimental import pallas as pl
from jax.experimental.pallas import tpu as pltpu
from jax.sharding import PartitionSpec as P

HEAD = 128
masked_score = -1e30
f32 = jnp.float32
bf16 = jnp.bfloat16


def dot_t(a, b):
    return lax.dot_general(a, b, (((1,), (1,)), ((), ())), preferred_element_type=f32)


def dot(a, b):
    return lax.dot_general(a, b, (((1,), (0,)), ((), ())), preferred_element_type=f32)


def twice(table):
    flat = table.reshape(-1, table.shape[-1])
    return jnp.concatenate([flat, flat], 0)


def row_iota(shape):
    return lax.broadcasted_iota(jnp.int32, shape, 0)


def lane_iota(shape):
    return lax.broadcasted_iota(jnp.int32, shape, 1)


def moved_in(base, rows, arrives):
    for r in range(rows.shape[0]):
        taken = arrives[r] > 0.5
        if base.shape[1] != taken.shape[1]:
            taken = jnp.concatenate([taken] * (base.shape[1] // taken.shape[1]), 1)
        base = jnp.where(taken, rows[r : r + 1], base)
    return base


def start_all(pairs, sems, first=0):
    copies = [pltpu.make_async_copy(src, dst, sems.at[first + n]) for n, (src, dst) in enumerate(pairs)]
    for copy in copies:
        copy.start()
    return copies


def wait_all(copies):
    for copy in copies:
        copy.wait()


def halves(value):
    high = value.astype(bf16).astype(f32)
    return jnp.concatenate([high, value - high], 0)


def stage_kernel(
    ids_at, counts_at, leave_at, land_at, lengths_at, h1, h2, q2, f2, tables_at,
    first_out, second_out, down_out, parcel_out, arrives_out, adapter_out, lengths_out,
    ids, counts, leave, land, lengths, fresh, fresh_wide, up, sems,
):
    me = lax.axis_index("inst")
    width = h1.shape[2]
    copies = start_all(
        [
            (f2.at[0], fresh), (h1.at[0], first_out),
            (h2.at[0], second_out.at[:, :width]), (q2.at[0], second_out.at[:, width : 2 * width]),
            (ids_at, ids), (counts_at, counts), (leave_at, leave), (land_at, land), (lengths_at, lengths),
            (tables_at.at[0, :, 0], down_out), (tables_at.at[0, :, 3], up),
        ],
        sems,
    )
    slots, lanes = adapter_out.shape
    rank = down_out.shape[1]
    wait_all(copies[:1])
    fresh_wide[...] = fresh[...].astype(f32)
    second_out[:, 2 * width : 2 * width + HEAD] = fresh_wide[:, 0, :].astype(bf16)
    second_out[:, 2 * width + HEAD :] = fresh_wide[:, 1, :].astype(bf16)
    wait_all(copies[4:9])
    row, lane = row_iota((slots, lanes)), lane_iota((slots, lanes))
    adapter = jnp.zeros((slots, lanes), jnp.int32)
    length = jnp.zeros((slots, lanes), jnp.int32)
    target = jnp.full((slots, lanes), -1, jnp.int32)
    for s in range(slots):
        adapter = jnp.where(row == s, ids[s, me], adapter)
        length = jnp.where(row == s, lengths[s, me], length)
    for m in range(leave.shape[0]):
        target = jnp.where((row == leave[m, me]) & (m < counts[me]), land[m, me], target)
    adapter_out[...] = jnp.where(lax.rem(lane, lanes // 2) // rank == adapter, 1.0, 0.0)
    lengths_out[...] = length
    for r in range(slots):
        arrives_out[r] = jnp.where(target == r, 1.0, 0.0)
    wait_all(copies[1:4] + copies[9:])
    ups = up[...].reshape(-1, width)
    parcel_out[: ups.shape[0]] = ups
    fresh_rows = second_out[:, 2 * width :].astype(f32)
    fresh_rows = jnp.concatenate([fresh_rows, jnp.zeros((slots, width - 2 * HEAD), f32)], 1)
    tail = jnp.concatenate([second_out[:, width : 2 * width].astype(f32), fresh_rows], 0)
    parcel_out[ups.shape[0] :] = tail.astype(bf16)


def rank_kernel(first, second, hidden_other, down, arrives, adapter, out):
    peers, slots, lanes = out.shape
    width = down.shape[2]
    hidden = [ref[:, :width].astype(f32) for ref in (first, second, hidden_other)]
    partials = dot_t(jnp.concatenate(hidden, 0).astype(bf16), twice(down[...]))
    moved = moved_in(partials[slots : 2 * slots], partials[2 * slots :], arrives)
    both = jnp.where(lane_iota((slots, lanes)) < lanes // 2, partials[:slots], moved)
    both = jnp.where(adapter[...] > 0.5, both, 0.0)
    for peer in range(peers):
        out[peer] = both


def attention_kernel(
    counts_at, leave_at, land_at, kv, ranks, base1, fresh1, second_rows, parcel, tables,
    arrives, adapter, lengths,
    attn1_out, own_out, landing_out, sums_out,
    counts, leave, land, queries, scores, mixed, served_rows, rank_rows, fresh_wide, sems,
):
    me = lax.axis_index("inst")
    half = lax.axis_size("inst") // 2
    slots, width = attn1_out.shape
    heads = width // HEAD
    cached = kv.shape[3]
    lanes = ranks.shape[2]
    moves = leave.shape[0]
    small = start_all([(counts_at, counts), (leave_at, leave), (land_at, land)], sems)

    lane = lane_iota((slots, lanes))
    low = lane < lanes // 2
    total = ranks[0]
    for peer in range(1, ranks.shape[0]):
        total = total + ranks[peer]
    total = jnp.concatenate([jnp.where(low, total, 0.0), jnp.where(low, 0.0, total)], 0).astype(bf16)
    update = dot(total, twice(tables[0, :, 1]))
    fresh_wide[...] = fresh1[0].astype(f32)
    own = second_rows[:, width:].astype(f32)
    got = parcel[pl.ds(parcel.shape[0] - 2 * slots, 2 * slots), :].astype(f32)
    second = moved_in(own, jnp.concatenate([got[:slots], got[slots:, : 2 * HEAD]], 1), arrives)
    query1 = (base1[0].astype(f32) + update[:slots]).astype(bf16).astype(f32)
    query2 = (second[:, :width] + update[slots:]).astype(bf16).astype(f32)
    for h in range(heads):
        columns = slice(h * HEAD, (h + 1) * HEAD)
        queries[h, :slots] = query1[:, columns]
        queries[h, slots:] = query2[:, columns]
    key1, value1 = fresh_wide[:, 0, :], fresh_wide[:, 1, :]
    key2, value2 = second[:, width : width + HEAD], second[:, width + HEAD :]

    scaling = math.log2(math.e) / math.sqrt(HEAD)
    score_shape = (2 * heads, cached)
    position = lane_iota(score_shape)
    extra = (position == cached - 2) | ((position == cached - 1) & (row_iota(score_shape) >= heads))
    last = pl.ds(cached - 16, 16)
    tail_row = row_iota((16, HEAD))

    def with_fresh(tile, one, two):
        tile = jnp.where(tail_row == 14, one, tile.astype(f32))
        return jnp.where(tail_row == 15, two, tile).astype(bf16)

    def with_tail(s, which, one, two):
        body = kv[0, s, which, : cached - 128]
        keep = kv[0, s, which, cached - 128 : cached - 16]
        return body, jnp.concatenate([keep, with_fresh(kv[0, s, which, last, :], one, two)], 0)

    for s in range(slots):
        body, tail = with_tail(s, 0, key1[s : s + 1], key2[s : s + 1])
        query = jnp.concatenate([queries[:, s, :], queries[:, slots + s, :]], 0).astype(bf16)
        score = dot_t(query, jnp.concatenate([body, tail], 0)) * scaling
        scores[s] = jnp.where((position < lengths[s : s + 1, :1]) | extra, score, masked_score)
    for s in range(slots):
        body, tail = with_tail(s, 1, value1[s : s + 1], value2[s : s + 1])
        score = scores[s]
        weights = jnp.exp2(score - jnp.max(score, 1, keepdims=True))
        probs = (weights * (1.0 / jnp.sum(weights, 1, keepdims=True))).astype(bf16)
        attended = dot(probs[:, : cached - 128], body) + dot(probs[:, cached - 128 :], tail)
        attended = attended.astype(bf16).astype(f32)
        mixed[s] = attended[:heads]
        mixed[slots + s] = attended[heads:]

    vacated = arrives[0]
    for r in range(1, slots):
        vacated = vacated + arrives[r]
    vacated = vacated > 0.5
    for h in range(heads):
        columns = slice(h * HEAD, (h + 1) * HEAD)
        served = mixed[slots:, h, :]
        served_rows[:slots, columns] = mixed[:slots, h, :]
        served_rows[slots : 2 * slots, columns] = jnp.where(vacated, own[:, width + HEAD :], served)
        served_rows[2 * slots :, columns] = served
    stacked = served_rows[...].astype(bf16)
    attn1_out[...] = served_rows[:slots].astype(bf16)
    own_out[...] = served_rows[slots : 2 * slots]

    partials = dot_t(stacked, twice(tables[0, :, 2]))
    mask = adapter[...] > 0.5
    for_own = jnp.where(mask, jnp.where(low, partials[:slots], partials[slots : 2 * slots]), 0.0)
    rank_rows[...] = jnp.where(mask, partials[2 * slots :], 0.0)
    for_other = jnp.zeros_like(for_own)
    row = row_iota((slots, lanes))
    wait_all(small)
    for m in range(moves):
        lands = (row == land[m, me]) & (m < counts[me])
        for_other = jnp.where(lands, rank_rows[pl.ds(leave[m, me], 1), :], for_other)
    peers = sums_out.shape[0] // 2
    lower = me < half
    for_own, for_other = halves(for_own), halves(for_other)
    in_low = jnp.where(lower, for_own, for_other).astype(bf16)
    in_high = jnp.where(lower, for_other, for_own).astype(bf16)
    sent = jnp.concatenate([mixed[slots + leave[m, me]] for m in range(moves)], 0).astype(bf16)
    for peer in range(peers):
        sums_out[peer, : 2 * slots] = in_low
        sums_out[peers + peer, : 2 * slots] = in_high
        sums_out[peer, 2 * slots :] = sent
        sums_out[peers + peer, 2 * slots :] = sent
    other = jnp.bitwise_xor(me, half)
    for m in range(moves):
        lands = (row == land[m, other]) & (m < counts[other])
        landing_out[m] = jnp.where(lands, 1.0, 0.0)


def delta_kernel(sums, tables, parcel, attn1, attn2_own, landing, attn1_out, delta1_out, attn2_out, delta2_out):
    attn1_out[...] = attn1[...]
    lower = lax.axis_index("inst") < lax.axis_size("inst") // 2
    peers = sums.shape[0] // 2
    lanes = sums.shape[2]
    slots, width = attn2_out.shape
    heads = width // HEAD
    moves = landing.shape[0]
    totals = []
    for part in range(2):
        total = sums[part * peers, : 2 * slots].astype(f32)
        for peer in range(1, peers):
            total = total + sums[part * peers + peer, : 2 * slots].astype(f32)
        totals.append(total[:slots] + total[slots:])
    own = jnp.where(lower, totals[0], totals[1])
    got = jnp.where(lower, totals[1], totals[0])
    low = lane_iota((slots, lanes)) < lanes // 2
    rank1 = jnp.where(low, own, 0.0)
    rank2_own = jnp.where(low, pltpu.roll(own, lanes // 2, 1), 0.0)
    rank2_got = jnp.where(low, 0.0, got)
    lands = [landing[m] > 0.5 for m in range(moves)]
    rank2 = rank2_own
    for m in range(moves):
        rank2 = jnp.where(lands[m], rank2_got, rank2)
    ups = tables[0, :, 3].reshape(-1, width)
    table = jnp.concatenate([ups, parcel[: ups.shape[0]]], 0)
    delta = dot(jnp.concatenate([rank1, rank2], 0).astype(bf16), table)
    delta1_out[...] = delta[:slots].astype(bf16)
    delta2_out[...] = delta[slots:].astype(bf16)
    mine = lax.axis_index("tensor")
    place = jnp.where(mine >= peers - 2, mine - (peers - 2), peers - 1 - mine)
    sender = jnp.where(lower, peers, 0) + place
    moved = sums[sender, 2 * slots :, :].astype(f32)
    for h in range(heads):
        columns = slice(h * HEAD, (h + 1) * HEAD)
        rows = attn2_own[:, columns]
        for m in range(moves):
            rows = jnp.where(lands[m], moved[m * heads + h : m * heads + h + 1], rows)
        attn2_out[:, columns] = rows.astype(bf16)


def per_device(
    query_first,
    query_second,
    hidden_first,
    hidden_second,
    fresh_first,
    fresh_second,
    kv_cache,
    adapters,
    lengths,
    adapter_ids,
    move_counts,
    move_from,
    move_to,
):
    inst_count = lax.axis_size("inst")
    peers = lax.axis_size("tensor")
    half = inst_count // 2
    swap = [(i, i ^ half) for i in range(inst_count)]
    teams = [[i * peers + t for t in reversed(range(peers))] for i in range(inst_count)]
    swapped = [team[1::-1] + team[2:] for team in teams]
    pairs = [swapped[i] + swapped[i + half] for i in range(half)]
    _, slots, width = query_first.shape
    _, pool, _, rank, _ = adapters.shape
    moves = move_from.shape[1]
    lanes = 2 * pool * rank
    heads = width // HEAD
    cached = kv_cache.shape[3]
    lengths, adapter_ids, move_from, move_to = lengths.T, adapter_ids.T, move_from.T, move_to.T

    hbm = pl.BlockSpec(memory_space=pltpu.HBM)
    vmem = pl.BlockSpec(memory_space=pltpu.VMEM)
    params = pltpu.CompilerParams(vmem_limit_bytes=16 * 1024 * 1024)

    def shape(dims, dtype):
        return jax.ShapeDtypeStruct(dims, dtype)

    def far(*arrays):
        return [pltpu.with_memory_space_constraint(array, pltpu.HBM) for array in arrays]

    def near(*arrays):
        return [pltpu.with_memory_space_constraint(array, pltpu.VMEM) for array in arrays]

    by_slot = pltpu.SMEM((slots, inst_count), jnp.int32)
    by_inst = pltpu.SMEM((inst_count,), jnp.int32)
    by_move = pltpu.SMEM((moves, inst_count), jnp.int32)
    rows = shape((slots, 2 * width + 2 * HEAD), bf16)

    first, second, down, parcel, arrives, adapter, slot_lengths = pl.pallas_call(
        stage_kernel,
        name="stage",
        out_shape=(
            shape((slots, width), bf16),
            rows,
            shape((pool, rank, width), bf16),
            shape((pool * rank + 2 * slots, width), bf16),
            shape((slots, slots, lanes), f32),
            shape((slots, lanes), f32),
            shape((slots, lanes), jnp.int32),
        ),
        in_specs=[hbm] * 10,
        out_specs=(vmem,) * 7,
        scratch_shapes=[
            by_slot, by_inst, by_move, by_move, by_slot,
            pltpu.VMEM((slots, 2, HEAD), bf16),
            pltpu.VMEM((slots, 2, HEAD), f32),
            pltpu.VMEM((pool, rank, width), bf16),
            pltpu.SemaphoreType.DMA((11,)),
        ],
        compiler_params=params,
    )(
        *far(
            adapter_ids, move_counts, move_from, move_to, lengths,
            hidden_first, hidden_second, query_second, fresh_second, adapters,
        )
    )
    parcel_other = lax.ppermute(parcel, "inst", swap)
    hidden_other = lax.ppermute(hidden_second[0], "inst", swap)

    ranks = pl.pallas_call(
        rank_kernel,
        name="rank_partials",
        out_shape=shape((peers, slots, lanes), f32),
        in_specs=[vmem] * 6,
        out_specs=vmem,
        cost_estimate=pl.CostEstimate(flops=2 * 10**10, bytes_accessed=10**8, transcendentals=0),
        compiler_params=params,
    )(*near(first, second, hidden_other, down, arrives, adapter))
    ranks = lax.all_to_all(ranks, ("inst", "tensor"), 0, 0, axis_index_groups=teams)

    attn1, attn2_own, landing, sums = pl.pallas_call(
        attention_kernel,
        name="attention",
        out_shape=(
            shape((slots, width), bf16),
            shape((slots, width), f32),
            shape((moves, slots, lanes), f32),
            shape((2 * peers, 2 * slots + moves * heads, lanes), bf16),
        ),
        in_specs=[hbm] * 3 + [vmem] * 10,
        out_specs=(vmem,) * 4,
        scratch_shapes=[
            by_inst, by_move, by_move,
            pltpu.VMEM((heads, 2 * slots, HEAD), f32),
            pltpu.VMEM((slots, 2 * heads, cached), f32),
            pltpu.VMEM((2 * slots, heads, HEAD), f32),
            pltpu.VMEM((3 * slots, width), f32),
            pltpu.VMEM((slots, lanes), f32),
            pltpu.VMEM((slots, 2, HEAD), f32),
            pltpu.SemaphoreType.DMA((3,)),
        ],
        compiler_params=params,
    )(
        *far(move_counts, move_from, move_to),
        *near(kv_cache, ranks, query_first, fresh_first, second, parcel_other, adapters, arrives, adapter, slot_lengths),
    )
    sums = lax.all_to_all(sums, ("inst", "tensor"), 0, 0, axis_index_groups=pairs)

    attn1, delta1, attn2, delta2 = pl.pallas_call(
        delta_kernel,
        name="deltas",
        out_shape=(shape((slots, width), bf16),) * 4,
        in_specs=[vmem] * 6,
        out_specs=(vmem,) * 4,
        compiler_params=params,
    )(*near(sums, adapters, parcel_other, attn1, attn2_own, landing))
    return (attn1[None], delta1[None], attn2[None], delta2[None])


def solution(mesh):
    row = P("inst", None, "tensor")
    fresh = P("inst", None, None, "tensor")
    whole = P("inst", None, None, None, "tensor")
    return jax.shard_map(
        per_device,
        mesh=mesh,
        in_specs=(row, row, row, row, fresh, fresh, whole, whole, P(), P(), P(), P(), P()),
        out_specs=(row, row, row, row),
        check_vma=False,
    )
```
